512 devices in a mesh: rows: 128 (over z, y, core), cols: 4 (over x).
Axes of the slice: x: 4, y: 8, z: 8, core: 2. Of those that a mesh axis runs over, the one named last changes fastest.
Arguments:
- basis_cols: bfloat16 [524288, 1024], P('rows', 'cols'), may hold values from -6 to 6, as said below
- snapshots: bfloat16 [256, 524288], P(None, 'rows'), may hold values from -600 to 600
Outputs:
- coefficients: float32 [1024, 256], P('cols')
- factor: float32 [256, 256], replicated
- directions: bfloat16 [256, 524288], P(None, ('rows', 'cols'))
The draws below stay inside these ranges and needn't reach their ends.
Inputs may be any that keep to these rules, and one draw needn't show every extreme that they name: `basis_cols`: normal entries.
All inputs are finite; a program needn't handle non-finite values.
Results may differ from the reference program's by a relative error of at most 0.0056.
Values may be sent and summed in bfloat16 or wider, within the bound.
A program may use at most 64 MiB of HBM per device.

```python
import math
import jax
import jax.numpy as jnp
from jax import lax

RANK = 1024
SNAPS = 256
M_DEV = 4096
M = 524288


def basis_block(key, index):
    sub = jax.random.fold_in(jax.random.fold_in(key, 7), index)
    return jnp.clip(jax.random.normal(sub, (M_DEV, RANK), jnp.float32), -6.0, 6.0)


def draw_basis_cols(key, part):
    blocks = lax.map(lambda index: basis_block(key, index).astype(jnp.bfloat16), jnp.arange(M // M_DEV))
    return blocks.reshape(M, RANK)


def draw_snapshots(key, part):
    amp_key = jax.random.fold_in(key, 11)
    amplitude = jax.random.normal(jax.random.fold_in(amp_key, 1), (RANK, SNAPS), jnp.float32)
    snap_scale = jnp.exp(jax.random.uniform(jax.random.fold_in(amp_key, 2), (SNAPS,), jnp.float32) * math.log(10.0))
    amplitude = amplitude * snap_scale[None, :]

    def one_block(index):
        lower = basis_block(key, index)
        signal = jnp.dot(lower, amplitude, precision=lax.Precision.HIGHEST) / math.sqrt(RANK)
        noise_key = jax.random.fold_in(jax.random.fold_in(key, 13), index)
        noise = jax.random.normal(noise_key, (M_DEV, SNAPS), jnp.float32)
        points = (index * M_DEV + jnp.arange(M_DEV)).astype(jnp.float32)
        row_key = jax.random.fold_in(jax.random.fold_in(key, 17), index)
        rise = jnp.exp(math.log(3.0) * points / M) * jnp.exp(jax.random.uniform(row_key, (M_DEV,), jnp.float32) * math.log(4.0))
        return (rise[:, None] * (signal + 0.5 * snap_scale[None, :] * noise)).T
    blocks = lax.map(one_block, jnp.arange(M // M_DEV))
    whole = jnp.transpose(blocks, (1, 0, 2)).reshape(SNAPS, M)
    return jnp.clip(whole, -600.0, 600.0).astype(jnp.bfloat16)


def setup_inputs(seed: int = 0) -> dict:
    streams_of = jax.random.split(jax.random.key(seed), 3)
    return {
        "basis_cols": draw_basis_cols(jax.random.fold_in(streams_of[2], 71), 0),
        "snapshots": draw_snapshots(jax.random.fold_in(streams_of[2], 71), 0),
    }


def reference(basis_cols, snapshots):
    raw = lax.dot_general(basis_cols.astype(jnp.float32), snapshots.astype(jnp.float32), (((0,), (1,)), ((), ())), preferred_element_type=jnp.float32)
    coefficients = raw * (math.sqrt(RANK) / M)
    coeff_low = coefficients.astype(jnp.bfloat16)
    recon = lax.dot_general(coeff_low.astype(jnp.float32), basis_cols.astype(jnp.float32), (((0,), (1,)), ((), ())), preferred_element_type=jnp.float32) / math.sqrt(RANK)
    residual = snapshots.astype(jnp.float32) - recon
    gram = jnp.dot(residual, residual.T, precision=lax.Precision.HIGHEST) / M
    factor = jnp.linalg.cholesky(gram)
    directions = lax.linalg.triangular_solve(factor, residual, left_side=True, lower=True).astype(jnp.bfloat16)
    return (coefficients, factor, directions)
```

```python
import functools
import math

import jax
import jax.numpy as jnp
from jax import lax
from jax.experimental import pallas as pl
from jax.experimental.pallas import tpu as pltpu
from jax.sharding import PartitionSpec as P

RANK = 1024
SIDE_Y = 8
MESH = pl.DeviceIdType.MESH
F32 = jnp.float32
BF16 = jnp.bfloat16
HALF = 128


def exchange(kernel_kernel, b_hbm, s_hbm, coef_o, gram_o, res_o, bv, sv, bfull, qfull, cbuf,
             pbuf, gbuf, core_in, rs_in, ar_in, x_in, part, ag, load_sem, bx_s, bx_r, qx_s, qx_r,
             qc_s, qc_r, cc_s, cc_r, core_s, core_r, rs_s, rs_r, ar_s, ar_r, ag_s, ag_r, x_s, x_r,
             gc_s, gc_r):
    ny, nz, nx, points = kernel_kernel
    row, x = lax.axis_index("rows"), lax.axis_index("cols")
    z, y, c = row // (2 * ny), (row // 2) % ny, row % 2
    own_points = b_hbm.shape[0] // nx

    def device(z, y, c, x):
        return ((z * ny + y) * 2 + c, x)

    def ring(me, n):
        return [lax.rem(me + k, n) for k in range(1, n)]

    y_peers, z_peers, x_peers = ring(y, ny), ring(z, nz), ring(x, nx)
    mate = device(z, y, 1 - c, x)

    first = ((y, ny, y_peers, lambda t: device(z, t, c, x)), (z, nz, z_peers, lambda t: device(t, y, c, x)))
    second = (first[1], first[0])

    def remote(src, dst, send, recv, dev):
        return pltpu.make_async_remote_copy(
            src_ref=src, dst_ref=dst, send_sem=send, recv_sem=recv, device_id=dev, device_id_type=MESH
        )

    load_b = pltpu.make_async_copy(b_hbm, bv, load_sem.at[0])
    load_s = pltpu.make_async_copy(s_hbm, sv, load_sem.at[1])
    load_b.start()
    load_s.start()

    barrier = pltpu.get_barrier_semaphore()
    peers = [mate] + [device(z, t, c, x) for t in y_peers] + [device(t, y, c, x) for t in z_peers]
    peers += [device(z, y, c, t) for t in x_peers]
    for peer in peers:
        pl.semaphore_signal(barrier, inc=1, device_id=peer, device_id_type=MESH)
    pl.semaphore_wait(barrier, len(peers))

    pending = []

    for t in x_peers:
        copy = remote(b_hbm.at[pl.ds(t * own_points, own_points)], bfull.at[x], bx_s.at[t], bx_r.at[x],
                      device(z, y, c, t))
        copy.start()
        pending.append(copy)
    load_own = pltpu.make_async_copy(b_hbm.at[pl.ds(x * own_points, own_points)], bfull.at[x], load_sem.at[2])
    load_own.start()

    load_b.wait()
    load_s.wait()
    steps = 4
    depth = b_hbm.shape[0] // steps
    total = None
    for k in range(steps):
        piece = jnp.dot(sv[:, k * depth:(k + 1) * depth], bv[k * depth:(k + 1) * depth, :],
                        preferred_element_type=F32)
        total = piece if total is None else total + piece

    def reduce(phase, buf, value, over_x):
        for h in range(2):
            for l in range(2):
                buf[h, l] = value[h * HALF:(h + 1) * HALF, l * HALF:(l + 1) * HALF]
        copy = remote(buf.at[1 - c], core_in.at[phase], core_s.at[phase], core_r.at[phase], mate)
        copy.start()
        pending.append(copy)
        copy.wait_recv()
        for l in range(2):
            me, n, ring_peers, dev = first[l]
            rows = HALF // n
            mine = buf[c, l] + core_in[phase, l]
            part[phase, 0, l] = mine
            for t in ring_peers:
                copy = remote(part.at[phase, 0, l, pl.ds(t * rows, rows)], rs_in.at[phase, l, me],
                              rs_s.at[phase, l, t], rs_r.at[phase, l, me], dev(t))
                copy.start()
                pending.append(copy)
            rs_in[phase, l, me] = part[phase, 0, l, pl.ds(pl.multiple_of(me * rows, rows), rows), :]
        for l in range(2):
            me, n, ring_peers, dev = first[l]
            for t in ring_peers:
                remote(rs_in.at[phase, l, t], rs_in.at[phase, l, t], rs_s.at[phase, l, t], rs_r.at[phase, l, t],
                       mate).wait_recv()
            got = rs_in[phase, l, 0]
            for i in range(1, n):
                got = got + rs_in[phase, l, i]
            me, n, ring_peers, dev = second[l]
            ar_in[phase, l, me] = got
            for t in ring_peers:
                copy = remote(ar_in.at[phase, l, me], ar_in.at[phase, l, me], ar_s.at[phase, l, t],
                              ar_r.at[phase, l, me], dev(t))
                copy.start()
                pending.append(copy)
        for l in range(2):
            me, n, ring_peers, dev = second[l]
            for t in ring_peers:
                remote(ar_in.at[phase, l, t], ar_in.at[phase, l, t], ar_s.at[phase, l, t], ar_r.at[phase, l, t],
                       mate).wait_recv()
            got = ar_in[phase, l, 0]
            for i in range(1, n):
                got = got + ar_in[phase, l, i]
            if over_x:
                x_in[x, l] = got
                for t in x_peers:
                    copy = remote(x_in.at[x, l], x_in.at[x, l], x_s.at[l, t], x_r.at[l, x], device(z, y, c, t))
                    copy.start()
                    pending.append(copy)
            else:
                me, n, ring_peers, dev = first[l]
                rows = HALF // n
                own = pl.ds(pl.multiple_of(me * rows, rows), rows)
                ag[phase, l, own, :] = got
        if over_x:
            for l in range(2):
                for t in x_peers:
                    remote(x_in.at[t, l], x_in.at[t, l], x_s.at[l, t], x_r.at[l, t], mate).wait_recv()
                got = x_in[0, l]
                for i in range(1, nx):
                    got = got + x_in[i, l]
                me, n, ring_peers, dev = first[l]
                rows = HALF // n
                own = pl.ds(pl.multiple_of(me * rows, rows), rows)
                ag[phase, l, own, :] = got
        for l in range(2):
            me, n, ring_peers, dev = first[l]
            rows = HALF // n
            own = pl.ds(pl.multiple_of(me * rows, rows), rows)
            for t in ring_peers:
                copy = remote(ag.at[phase, l, own], ag.at[phase, l, own], ag_s.at[phase, l, t],
                              ag_r.at[phase, l, me], dev(t))
                copy.start()
                pending.append(copy)
        for l in range(2):
            me, n, ring_peers, dev = first[l]
            rows = HALF // n
            for t in ring_peers:
                theirs = ag.at[phase, l, pl.ds(t * rows, rows)]
                remote(theirs, theirs, ag_s.at[phase, l, t], ag_r.at[phase, l, t], mate).wait_recv()

    reduce(0, pbuf, total, False)

    scale = math.sqrt(RANK) / points
    own = jnp.concatenate([ag[0, 0], ag[0, 1]], axis=1) * scale
    qfull[x, c] = own.astype(BF16)
    for t in x_peers:
        copy = remote(qfull.at[x, c], qfull.at[x, c], qx_s.at[t], qx_r.at[x], device(z, y, c, t))
        copy.start()
        pending.append(copy)
    cbuf[c] = own

    def to_mate(t):
        copy = remote(qfull.at[t, c], qfull.at[t, c], qc_s.at[t], qc_r.at[t], mate)
        copy.start()
        pending.append(copy)

    to_mate(x)
    copy = remote(cbuf.at[c], cbuf.at[c], cc_s, cc_r, mate)
    copy.start()
    pending.append(copy)
    for t in x_peers:
        remote(qfull.at[t, c], qfull.at[t, c], qx_s.at[t], qx_r.at[t], mate).wait_recv()
        to_mate(t)
    for t in range(nx):
        remote(qfull.at[t, 1 - c], qfull.at[t, 1 - c], qc_s.at[t], qc_r.at[t], mate).wait_recv()

    load_own.wait()
    for t in x_peers:
        remote(bfull.at[t], bfull.at[t], bx_s.at[t], bx_r.at[t], mate).wait_recv()
    recon = None
    for t in range(nx):
        piece = lax.dot_general(qfull[t].reshape(2 * HALF, 2 * HALF), bfull[t], (((1,), (1,)), ((), ())),
                                preferred_element_type=F32)
        recon = piece if recon is None else recon + piece
    own_snaps = sv[:, pl.ds(pl.multiple_of(x * own_points, own_points), own_points)].astype(F32)
    residual = own_snaps - recon * (1.0 / math.sqrt(RANK))
    res_o[...] = residual
    gram = lax.dot_general(residual, residual, (((1,), (1,)), ((), ())), precision=lax.Precision.HIGHEST,
                           preferred_element_type=F32) * (1.0 / points)
    reduce(1, gbuf, gram, True)
    gc = remote(ag.at[1], gbuf.at[2], gc_s, gc_r, mate)
    gc.start()
    pending.append(gc)
    remote(cbuf.at[1 - c], cbuf.at[1 - c], cc_s, cc_r, mate).wait_recv()
    for h in range(2):
        coef_o[:, h * HALF:(h + 1) * HALF] = cbuf[h].T
    rows_own = pl.ds(pl.multiple_of(c * HALF, HALF), HALF)
    rows_mate = pl.ds(pl.multiple_of((1 - c) * HALF, HALF), HALF)
    gram_o[rows_own, :] = jnp.concatenate([ag[1, 0], ag[1, 1]], axis=1)
    gc.wait_recv()
    gram_o[rows_mate, :] = jnp.concatenate([gbuf[2, 0], gbuf[2, 1]], axis=1)
    for copy in pending:
        copy.wait_send()


def shards(sides, basis_cols, snapshots):
    ny, nz, nx, points = sides
    own_points = basis_cols.shape[0] // nx
    modes = basis_cols.shape[1]
    snaps = snapshots.shape[0]
    n = max(ny, nz)
    dma = pltpu.SemaphoreType.DMA
    chunk = HALF // n
    coefficients, gram, residual = pl.pallas_call(
        functools.partial(exchange, sides),
        out_shape=(
            jax.ShapeDtypeStruct((modes, snaps), F32),
            jax.ShapeDtypeStruct((snaps, snaps), F32),
            jax.ShapeDtypeStruct((snaps, own_points), F32),
        ),
        in_specs=[pl.BlockSpec(memory_space=pl.ANY)] * 2,
        out_specs=(pl.BlockSpec(memory_space=pltpu.VMEM),) * 3,
        scratch_shapes=[
            pltpu.VMEM(basis_cols.shape, BF16),
            pltpu.VMEM(snapshots.shape, BF16),
            pltpu.VMEM((nx, own_points, modes), BF16),
            pltpu.VMEM((nx, 2, HALF, modes), BF16),
            pltpu.VMEM((2, HALF, modes), F32),
            pltpu.VMEM((2, 2, HALF, HALF), F32),
            pltpu.VMEM((3, 2, HALF, HALF), F32),
            pltpu.VMEM((2, 2, HALF, HALF), F32),
            pltpu.VMEM((2, 2, n, chunk, HALF), F32),
            pltpu.VMEM((2, 2, n, chunk, HALF), F32),
            pltpu.VMEM((nx, 2, chunk, HALF), F32),
            pltpu.VMEM((2, 1, 2, HALF, HALF), F32),
            pltpu.VMEM((2, 2, HALF, HALF), F32),
            dma((3,)),
            dma((nx,)), dma((nx,)),
            dma((nx,)), dma((nx,)),
            dma((nx,)), dma((nx,)),
            dma(()), dma(()),
            dma((2,)), dma((2,)),
            dma((2, 2, n)), dma((2, 2, n)),
            dma((2, 2, n)), dma((2, 2, n)),
            dma((2, 2, n)), dma((2, 2, n)),
            dma((2, nx)), dma((2, nx)),
            dma(()), dma(()),
        ],
        compiler_params=pltpu.CompilerParams(
            collective_id=0, has_side_effects=True, vmem_limit_bytes=48 << 20
        ),
        name="exchange",
    )(basis_cols, snapshots)
    factor = jnp.linalg.cholesky(gram)
    directions = lax.linalg.triangular_solve(factor, residual, left_side=True, lower=True).astype(BF16)
    return (coefficients, factor, directions)


def solution(mesh):
    rows, cols = mesh.shape["rows"], mesh.shape["cols"]
    placed = (P("rows", "cols"), P(None, "rows"))

    def whole(basis_cols, snapshots):
        sides = (SIDE_Y, rows // (2 * SIDE_Y), cols, basis_cols.shape[0])
        return jax.shard_map(
            functools.partial(shards, sides),
            mesh=mesh,
            in_specs=placed,
            out_specs=(P("cols", None), P(), P(None, ("rows", "cols"))),
            check_vma=False,
        )(basis_cols, snapshots)

    return whole
```

```python
import functools
import math

import jax
import jax.numpy as jnp
from jax import lax
from jax.experimental import pallas as pl
from jax.experimental.pallas import tpu as pltpu
from jax.sharding import PartitionSpec as P

RANK = 1024
SIDE_Y = 8
MESH = pl.DeviceIdType.MESH
F32 = jnp.float32
BF16 = jnp.bfloat16
HALF = 128


def exchange(sides, b_hbm, s_hbm, coef_o, gram_o, res_o, bv, sv, bfull, qfull, cbuf,
             pbuf, gbuf, core_in, rs_in, ar_in, x_in, part, ag, load_sem, bx_s, bx_r, qx_s, qx_r,
             qc_s, qc_r, cc_s, cc_r, core_s, core_r, rs_s, rs_r, ar_s, ar_r, ag_s, ag_r, x_s, x_r,
             gc_s, gc_r):
    ny, nz, nx, points = sides
    row, x = lax.axis_index("rows"), lax.axis_index("cols")
    z, y, c = row // (2 * ny), (row // 2) % ny, row % 2
    own_points = b_hbm.shape[0] // nx

    def device(z, y, c, x):
        return ((z * ny + y) * 2 + c, x)

    def ring(me, n):
        return [lax.rem(me + k, n) for k in range(1, n)]

    y_peers, z_peers, x_peers = ring(y, ny), ring(z, nz), ring(x, nx)
    mate = device(z, y, 1 - c, x)

    first = ((y, ny, y_peers, lambda t: device(z, t, c, x)), (z, nz, z_peers, lambda t: device(t, y, c, x)))
    second = (first[1], first[0])

    def remote(src, dst, send, recv, dev):
        return pltpu.make_async_remote_copy(
            src_ref=src, dst_ref=dst, send_sem=send, recv_sem=recv, device_id=dev, device_id_type=MESH
        )

    load_b = pltpu.make_async_copy(b_hbm, bv, load_sem.at[0])
    load_s = pltpu.make_async_copy(s_hbm, sv, load_sem.at[1])
    load_b.start()
    load_s.start()

    barrier = pltpu.get_barrier_semaphore()
    peers = [mate] + [device(z, t, c, x) for t in y_peers] + [device(t, y, c, x) for t in z_peers]
    peers += [device(z, y, c, t) for t in x_peers]
    for peer in peers:
        pl.semaphore_signal(barrier, inc=1, device_id=peer, device_id_type=MESH)
    pl.semaphore_wait(barrier, len(peers))

    pending = []

    for t in x_peers:
        copy = remote(b_hbm.at[pl.ds(t * own_points, own_points)], bfull.at[x], bx_s.at[t], bx_r.at[x],
                      device(z, y, c, t))
        copy.start()
        pending.append(copy)
    load_own = pltpu.make_async_copy(b_hbm.at[pl.ds(x * own_points, own_points)], bfull.at[x], load_sem.at[2])
    load_own.start()

    load_b.wait()
    load_s.wait()
    steps = 4
    depth = b_hbm.shape[0] // steps
    total = None
    for k in range(steps):
        piece = jnp.dot(sv[:, k * depth:(k + 1) * depth], bv[k * depth:(k + 1) * depth, :],
                        preferred_element_type=F32)
        total = piece if total is None else total + piece

    def reduce(phase, buf, value, over_x):
        for h in range(2):
            for l in range(2):
                buf[h, l] = value[h * HALF:(h + 1) * HALF, l * HALF:(l + 1) * HALF]
        copy = remote(buf.at[1 - c], core_in.at[phase], core_s.at[phase], core_r.at[phase], mate)
        copy.start()
        pending.append(copy)
        copy.wait_recv()
        for l in range(2):
            me, n, ring_peers, dev = first[l]
            rows = HALF // n
            mine = buf[c, l] + core_in[phase, l]
            part[phase, 0, l] = mine
            for t in ring_peers:
                copy = remote(part.at[phase, 0, l, pl.ds(t * rows, rows)], rs_in.at[phase, l, me],
                              rs_s.at[phase, l, t], rs_r.at[phase, l, me], dev(t))
                copy.start()
                pending.append(copy)
            rs_in[phase, l, me] = part[phase, 0, l, pl.ds(pl.multiple_of(me * rows, rows), rows), :]
        for l in range(2):
            me, n, ring_peers, dev = first[l]
            for t in ring_peers:
                remote(rs_in.at[phase, l, t], rs_in.at[phase, l, t], rs_s.at[phase, l, t], rs_r.at[phase, l, t],
                       mate).wait_recv()
            got = rs_in[phase, l, 0]
            for i in range(1, n):
                got = got + rs_in[phase, l, i]
            me, n, ring_peers, dev = second[l]
            ar_in[phase, l, me] = got
            for t in ring_peers:
                copy = remote(ar_in.at[phase, l, me], ar_in.at[phase, l, me], ar_s.at[phase, l, t],
                              ar_r.at[phase, l, me], dev(t))
                copy.start()
                pending.append(copy)
        for l in range(2):
            me, n, ring_peers, dev = second[l]
            for t in ring_peers:
                remote(ar_in.at[phase, l, t], ar_in.at[phase, l, t], ar_s.at[phase, l, t], ar_r.at[phase, l, t],
                       mate).wait_recv()
            got = ar_in[phase, l, 0]
            for i in range(1, n):
                got = got + ar_in[phase, l, i]
            if over_x:
                x_in[x, l] = got
                for t in x_peers:
                    copy = remote(x_in.at[x, l], x_in.at[x, l], x_s.at[l, t], x_r.at[l, x], device(z, y, c, t))
                    copy.start()
                    pending.append(copy)
            else:
                me, n, ring_peers, dev = first[l]
                rows = HALF // n
                own = pl.ds(pl.multiple_of(me * rows, rows), rows)
                ag[phase, l, own, :] = got
        if over_x:
            for l in range(2):
                for t in x_peers:
                    remote(x_in.at[t, l], x_in.at[t, l], x_s.at[l, t], x_r.at[l, t], mate).wait_recv()
                got = x_in[0, l]
                for i in range(1, nx):
                    got = got + x_in[i, l]
                me, n, ring_peers, dev = first[l]
                rows = HALF // n
                own = pl.ds(pl.multiple_of(me * rows, rows), rows)
                ag[phase, l, own, :] = got
        for l in range(2):
            me, n, ring_peers, dev = first[l]
            rows = HALF // n
            own = pl.ds(pl.multiple_of(me * rows, rows), rows)
            for t in ring_peers:
                copy = remote(ag.at[phase, l, own], ag.at[phase, l, own], ag_s.at[phase, l, t],
                              ag_r.at[phase, l, me], dev(t))
                copy.start()
                pending.append(copy)
        for l in range(2):
            me, n, ring_peers, dev = first[l]
            rows = HALF // n
            for t in ring_peers:
                theirs = ag.at[phase, l, pl.ds(t * rows, rows)]
                remote(theirs, theirs, ag_s.at[phase, l, t], ag_r.at[phase, l, t], mate).wait_recv()

    reduce(0, pbuf, total, False)

    scale = math.sqrt(RANK) / points
    own = jnp.concatenate([ag[0, 0], ag[0, 1]], axis=1) * scale
    qfull[x, c] = own.astype(BF16)
    for t in x_peers:
        copy = remote(qfull.at[x, c], qfull.at[x, c], qx_s.at[t], qx_r.at[x], device(z, y, c, t))
        copy.start()
        pending.append(copy)
    cbuf[c] = own

    def to_mate(t):
        copy = remote(qfull.at[t, c], qfull.at[t, c], qc_s.at[t], qc_r.at[t], mate)
        copy.start()
        pending.append(copy)

    to_mate(x)
    copy = remote(cbuf.at[c], cbuf.at[c], cc_s, cc_r, mate)
    copy.start()
    pending.append(copy)
    for t in x_peers:
        remote(qfull.at[t, c], qfull.at[t, c], qx_s.at[t], qx_r.at[t], mate).wait_recv()
        to_mate(t)
    for t in range(nx):
        remote(qfull.at[t, 1 - c], qfull.at[t, 1 - c], qc_s.at[t], qc_r.at[t], mate).wait_recv()

    load_own.wait()
    for t in x_peers:
        remote(bfull.at[t], bfull.at[t], bx_s.at[t], bx_r.at[t], mate).wait_recv()
    recon = None
    for t in range(nx):
        piece = lax.dot_general(qfull[t].reshape(2 * HALF, 2 * HALF), bfull[t], (((1,), (1,)), ((), ())),
                                preferred_element_type=F32)
        recon = piece if recon is None else recon + piece
    own_snaps = sv[:, pl.ds(pl.multiple_of(x * own_points, own_points), own_points)].astype(F32)
    residual = own_snaps - recon * (1.0 / math.sqrt(RANK))
    res_o[...] = residual
    gram = lax.dot_general(residual, residual, (((1,), (1,)), ((), ())), precision=lax.Precision.HIGHEST,
                           preferred_element_type=F32) * (1.0 / points)
    reduce(1, gbuf, gram, True)
    gc = remote(ag.at[1], gbuf.at[2], gc_s, gc_r, mate)
    gc.start()
    pending.append(gc)
    remote(cbuf.at[1 - c], cbuf.at[1 - c], cc_s, cc_r, mate).wait_recv()
    for h in range(2):
        coef_o[:, h * HALF:(h + 1) * HALF] = cbuf[h].T
    rows_own = pl.ds(pl.multiple_of(c * HALF, HALF), HALF)
    rows_mate = pl.ds(pl.multiple_of((1 - c) * HALF, HALF), HALF)
    gram_o[rows_own, :] = jnp.concatenate([ag[1, 0], ag[1, 1]], axis=1)
    gc.wait_recv()
    gram_o[rows_mate, :] = jnp.concatenate([gbuf[2, 0], gbuf[2, 1]], axis=1)
    for copy in pending:
        copy.wait_send()


def eliminate(a, n):
    lanes = 2 * n
    count = n // 8
    r_io = lax.broadcasted_iota(jnp.int32, (8, n), 0)
    c_io = lax.broadcasted_iota(jnp.int32, (8, n), 1)
    sub = lax.broadcasted_iota(jnp.int32, (8, lanes), 0)
    tiles = [jnp.concatenate([a[8 * t:8 * t + 8], jnp.where(c_io == r_io + 8 * t, 1.0, 0.0).astype(F32)], axis=1)
             for t in range(count)]
    def wide(v):
        return v if lanes == 128 else jnp.concatenate([v] * (lanes // 128), axis=1)
    for g in range(count):
        cols = {t: [jnp.broadcast_to(tiles[t][:, 8 * g + k:8 * g + k + 1], (8, 128)) for k in range(8)]
                for t in range(g, count)}
        piv = [[jnp.broadcast_to(cols[g][b][i:i + 1, :], (8, 128)) for b in range(i + 1)] for i in range(8)]
        rows = [jnp.broadcast_to(tiles[g][k:k + 1, :], (8, lanes)) for k in range(8)]
        for k in range(8):
            d = lax.rsqrt(piv[k][k])
            low = {i: piv[i][k] * d for i in range(k + 1, 8)}
            for i in range(k + 1, 8):
                for b in range(k + 1, i + 1):
                    piv[i][b] = piv[i][b] - low[i] * low[b]
            rows[k] = rows[k] * wide(d)
            for i in range(k + 1, 8):
                rows[i] = rows[i] - wide(low[i]) * rows[k]
            for t in range(g + 1, count):
                cols[t][k] = cols[t][k] * d
                for i in range(k + 1, 8):
                    cols[t][i] = cols[t][i] - low[i] * cols[t][k]
                tiles[t] = tiles[t] - wide(cols[t][k]) * rows[k]
        new = rows[0]
        for k in range(1, 8):
            new = jnp.where(sub == k, rows[k], new)
        tiles[g] = new
    w = jnp.concatenate(tiles, axis=0)
    return w[:, :n], w[:, n:]


def split(v):
    hi = v.astype(BF16)
    return hi, (v - hi.astype(F32)).astype(BF16)


def mm(a, b, dims):
    ah, al = split(a); bh, bl = split(b)
    dot = lambda p, q: lax.dot_general(p, q, (dims, ((), ())), preferred_element_type=F32)
    return dot(ah, bh) + (dot(ah, bl) + dot(al, bh))


def hi(a, b, dims):
    return lax.dot_general(a, b, (dims, ((), ())), precision=lax.Precision.HIGHEST, preferred_element_type=F32)


def factor_kernel(n, g_ref, r_ref, l_ref, d_ref, w):
    m = g_ref.shape[0]
    nb = m // n
    w[...] = g_ref[...]
    r_io = lax.broadcasted_iota(jnp.int32, (n, n), 0)
    c_io = lax.broadcasted_iota(jnp.int32, (n, n), 1)
    xs = []; ups = {}
    for k in range(nb):
        s = slice(k * n, (k + 1) * n)
        u, v = eliminate(w[s, s], n)
        l_ref[s, s] = jnp.where(r_io >= c_io, u.T, 0.0)
        if k + 1 < nb:
            rest = slice((k + 1) * n, m)
            up = hi(v, w[s, rest], ((1,), (0,)))
            w[rest, rest] = w[rest, rest] - hi(up, up, ((0,), (0,)))
            l_ref[rest, s] = up.T
            l_ref[s, rest] = jnp.zeros((n, m - (k + 1) * n), F32)
            ups[k] = up
        acc = r_ref[s, :]
        for j in range(k):
            acc = acc - mm(ups[j][:, (k - j - 1) * n:(k - j) * n], xs[j], ((0,), (0,)))
        x = mm(v, acc, ((1,), (0,)))
        xs.append(x)
        d_ref[s, :] = x.astype(BF16)


def shards(sides, basis_cols, snapshots):
    ny, nz, nx, points = sides
    own_points = basis_cols.shape[0] // nx
    modes = basis_cols.shape[1]
    snaps = snapshots.shape[0]
    n = max(ny, nz)
    dma = pltpu.SemaphoreType.DMA
    chunk = HALF // n
    coefficients, gram, residual = pl.pallas_call(
        functools.partial(exchange, sides),
        out_shape=(
            jax.ShapeDtypeStruct((modes, snaps), F32),
            jax.ShapeDtypeStruct((snaps, snaps), F32),
            jax.ShapeDtypeStruct((snaps, own_points), F32),
        ),
        in_specs=[pl.BlockSpec(memory_space=pltpu.HBM)] * 2,
        out_specs=(pl.BlockSpec(memory_space=pltpu.VMEM),) * 3,
        scratch_shapes=[
            pltpu.VMEM(basis_cols.shape, BF16),
            pltpu.VMEM(snapshots.shape, BF16),
            pltpu.VMEM((nx, own_points, modes), BF16),
            pltpu.VMEM((nx, 2, HALF, modes), BF16),
            pltpu.VMEM((2, HALF, modes), F32),
            pltpu.VMEM((2, 2, HALF, HALF), F32),
            pltpu.VMEM((3, 2, HALF, HALF), F32),
            pltpu.VMEM((2, 2, HALF, HALF), F32),
            pltpu.VMEM((2, 2, n, chunk, HALF), F32),
            pltpu.VMEM((2, 2, n, chunk, HALF), F32),
            pltpu.VMEM((nx, 2, chunk, HALF), F32),
            pltpu.VMEM((2, 1, 2, HALF, HALF), F32),
            pltpu.VMEM((2, 2, HALF, HALF), F32),
            dma((3,)),
            dma((nx,)), dma((nx,)),
            dma((nx,)), dma((nx,)),
            dma((nx,)), dma((nx,)),
            dma(()), dma(()),
            dma((2,)), dma((2,)),
            dma((2, 2, n)), dma((2, 2, n)),
            dma((2, 2, n)), dma((2, 2, n)),
            dma((2, 2, n)), dma((2, 2, n)),
            dma((2, nx)), dma((2, nx)),
            dma(()), dma(()),
        ],
        compiler_params=pltpu.CompilerParams(
            collective_id=0, has_side_effects=True, vmem_limit_bytes=60 << 20
        ),
        name="exchange",
    )(basis_cols, snapshots)
    factor, directions = pl.pallas_call(
        functools.partial(factor_kernel, 64),
        out_shape=(
            jax.ShapeDtypeStruct((snaps, snaps), F32),
            jax.ShapeDtypeStruct((snaps, own_points), BF16),
        ),
        scratch_shapes=[pltpu.VMEM((snaps, snaps), F32)],
        compiler_params=pltpu.CompilerParams(vmem_limit_bytes=32 << 20),
        name="factor",
    )(gram, residual)
    return (coefficients, factor, directions)


def solution(mesh):
    rows, cols = mesh.shape["rows"], mesh.shape["cols"]
    placed = (P("rows", "cols"), P(None, "rows"))

    def whole(basis_cols, snapshots):
        sides = (SIDE_Y, rows // (2 * SIDE_Y), cols, basis_cols.shape[0])
        return jax.shard_map(
            functools.partial(shards, sides),
            mesh=mesh,
            in_specs=placed,
            out_specs=(P("cols", None), P(), P(None, ("rows", "cols"))),
            check_vma=False,
        )(basis_cols, snapshots)

    return whole
```

```python
import functools
import math

import jax
import jax.numpy as jnp
from jax import lax
from jax.experimental import pallas as pl
from jax.experimental.pallas import tpu as pltpu
from jax.sharding import PartitionSpec as P

RANK = 1024
SIDE_Y = 8
MESH = pl.DeviceIdType.MESH
F32 = jnp.float32
BF16 = jnp.bfloat16
HALF = 128


def exchange(sides, b_hbm, s_hbm, coef_o, gram_o, res_o, bv, sv, bfull, qfull, cbuf, pbuf, pbuf2, gbuf,
             core_in, part, rs_in, ar_in, x_in, load_sem, bx_s, bx_r, core_s, core_r, rs_s, rs_r, ar_s, ar_r, x_s, x_r,
             ag_s, ag_r, out_s, out_r, cag_s, cag_r, cout_s, cout_r):
    ny, nz, nx, points = sides
    row, x = lax.axis_index("rows"), lax.axis_index("cols")
    z, y, c = row // (2 * ny), (row // 2) % ny, row % 2
    own_points = b_hbm.shape[0] // nx
    ring = ny
    rows = HALF // ring

    def device(z, y, c, x):
        return ((z * ny + y) * 2 + c, x)

    mate = device(z, y, 1 - c, x)
    far = sorted(range(1, ring), key=lambda k: -min(k, ring - k))
    one, two = jnp.where(c == 0, y, z), jnp.where(c == 0, z, y)
    one_peers = [lax.rem(one + k, ring) for k in far]
    two_peers = [lax.rem(two + k, ring) for k in far]
    x_peers = [lax.rem(x + k, nx) for k in sorted(range(1, nx), key=lambda k: -min(k, nx - k))]

    def along_one(t):
        return device(jnp.where(c == 0, z, t), jnp.where(c == 0, t, y), c, x)

    def along_two(t):
        return device(jnp.where(c == 0, t, z), jnp.where(c == 0, y, t), c, x)

    def along_x(t):
        return device(z, y, c, t)

    def remote(src, dst, send, recv, dev):
        return pltpu.make_async_remote_copy(
            src_ref=src, dst_ref=dst, send_sem=send, recv_sem=recv, device_id=dev, device_id_type=MESH
        )

    pending = []

    def send(*args):
        copy = remote(*args)
        copy.start()
        pending.append(copy)

    def arrived(ref, sem):
        remote(ref, ref, load_sem.at[3], sem, mate).wait_recv()

    load_b = pltpu.make_async_copy(b_hbm, bv, load_sem.at[0])
    load_s = pltpu.make_async_copy(s_hbm, sv, load_sem.at[1])
    load_b.start()
    load_s.start()

    barrier = pltpu.get_barrier_semaphore()
    peers = [mate] + [along_one(t) for t in one_peers] + [along_two(t) for t in two_peers]
    peers += [along_x(t) for t in x_peers]
    for peer in peers:
        pl.semaphore_signal(barrier, inc=1, device_id=peer, device_id_type=MESH)
    pl.semaphore_wait(barrier, len(peers))

    for t in x_peers:
        send(b_hbm.at[pl.ds(t * own_points, own_points)], bfull.at[x], bx_s.at[t], bx_r.at[x], along_x(t))
    load_own = pltpu.make_async_copy(b_hbm.at[pl.ds(x * own_points, own_points)], bfull.at[x], load_sem.at[2])
    load_own.start()

    load_b.wait()
    load_s.wait()
    steps = 4
    depth = b_hbm.shape[0] // steps
    total = None
    for k in range(steps):
        piece = jnp.dot(sv[:, k * depth:(k + 1) * depth], bv[k * depth:(k + 1) * depth, :],
                        preferred_element_type=F32)
        total = piece if total is None else total + piece

    chunk = pl.ds(pl.multiple_of(one * rows, rows), rows)
    half = pl.ds(pl.multiple_of(c * HALF, HALF), HALF)
    other = pl.ds(pl.multiple_of((1 - c) * HALF, HALF), HALF)

    def half_chunk(t):
        return pl.ds(pl.multiple_of(c * HALF + t * rows, rows), rows)

    def row_sum(phase, buf, value):
        buf[...] = value
        send(buf.at[other], core_in.at[phase], core_s.at[phase], core_r.at[phase], mate)
        arrived(core_in.at[phase], core_r.at[phase])
        part[phase] = buf[half, :] + core_in[phase]
        for t in one_peers:
            send(part.at[phase, pl.ds(pl.multiple_of(t * rows, rows), rows)], rs_in.at[phase, one],
                 rs_s.at[phase, t], rs_r.at[phase, one], along_one(t))
        rs_in[phase, one] = part[phase, chunk, :]
        for t in one_peers:
            arrived(rs_in.at[phase, t], rs_r.at[phase, t])
        got = rs_in[phase, 0]
        for i in range(1, ring):
            got = got + rs_in[phase, i]
        ar_in[phase, two] = got
        for t in two_peers:
            send(ar_in.at[phase, two], ar_in.at[phase, two], ar_s.at[phase, t], ar_r.at[phase, two], along_two(t))
        for t in two_peers:
            arrived(ar_in.at[phase, t], ar_r.at[phase, t])
        got = ar_in[phase, 0]
        for i in range(1, ring):
            got = got + ar_in[phase, i]
        return got

    own = row_sum(0, pbuf, total) * (math.sqrt(RANK) / points)
    mine = half_chunk(one)
    qfull[x, mine, :] = own.astype(BF16)
    for t in x_peers:
        send(qfull.at[x, mine], qfull.at[x, mine], x_s.at[0, t], x_r.at[0, x], along_x(t))
    cbuf[mine, :] = own
    for t in x_peers:
        arrived(qfull.at[t, mine], x_r.at[0, t])
    for t in one_peers:
        send(qfull.at[:, mine], qfull.at[:, mine], ag_s.at[0, t], ag_r.at[0, one], along_one(t))
    for t in one_peers:
        send(cbuf.at[mine], cbuf.at[mine], cag_s.at[t], cag_r.at[one], along_one(t))
    for t in one_peers:
        arrived(qfull.at[:, half_chunk(t)], ag_r.at[0, t])
    send(qfull.at[:, half], qfull.at[:, half], out_s.at[0], out_r.at[0], mate)
    for t in one_peers:
        arrived(cbuf.at[half_chunk(t)], cag_r.at[t])
    send(cbuf.at[half], cbuf.at[half], cout_s, cout_r, mate)
    arrived(qfull.at[:, other], out_r.at[0])

    def from_modes(t):
        return lax.dot_general(qfull[t], bfull[t], (((1,), (1,)), ((), ())), preferred_element_type=F32)

    load_own.wait()
    recon = from_modes(x)
    for t in reversed(x_peers):
        arrived(bfull.at[t], bx_r.at[t])
        recon = recon + from_modes(t)
    own_snaps = sv[:, pl.ds(pl.multiple_of(x * own_points, own_points), own_points)].astype(F32)
    residual = own_snaps - recon * (1.0 / math.sqrt(RANK))
    gram = lax.dot_general(residual, residual, (((1,), (1,)), ((), ())), precision=lax.Precision.HIGHEST,
                           preferred_element_type=F32) * (1.0 / points)
    res_o[...] = residual
    got = row_sum(1, pbuf2, gram)
    x_in[x] = got
    for t in x_peers:
        send(x_in.at[x], x_in.at[x], x_s.at[1, t], x_r.at[1, x], along_x(t))
    arrived(cbuf.at[other], cout_r)
    coef_o[...] = cbuf[...].T
    for t in x_peers:
        arrived(x_in.at[t], x_r.at[1, t])
    got = x_in[0]
    for i in range(1, nx):
        got = got + x_in[i]
    gbuf[mine, :] = got
    for t in one_peers:
        send(gbuf.at[mine], gbuf.at[mine], ag_s.at[1, t], ag_r.at[1, one], along_one(t))
    for t in one_peers:
        arrived(gbuf.at[half_chunk(t)], ag_r.at[1, t])
    send(gbuf.at[half], gbuf.at[half], out_s.at[1], out_r.at[1], mate)
    gram_o[half, :] = gbuf[half, :]
    arrived(gbuf.at[other], out_r.at[1])
    gram_o[other, :] = gbuf[other, :]
    for copy in pending:
        copy.wait_send()


def eliminate(a, n):
    lanes = 2 * n
    count = n // 8
    r_io = lax.broadcasted_iota(jnp.int32, (8, n), 0)
    c_io = lax.broadcasted_iota(jnp.int32, (8, n), 1)
    sub = lax.broadcasted_iota(jnp.int32, (8, lanes), 0)
    tiles = [jnp.concatenate([a[8 * t:8 * t + 8], jnp.where(c_io == r_io + 8 * t, 1.0, 0.0).astype(F32)], axis=1)
             for t in range(count)]
    def wide(v):
        return v if lanes == 128 else jnp.concatenate([v] * (lanes // 128), axis=1)
    for g in range(count):
        cols = {t: [jnp.broadcast_to(tiles[t][:, 8 * g + k:8 * g + k + 1], (8, 128)) for k in range(8)]
                for t in range(g, count)}
        piv = [[jnp.broadcast_to(cols[g][b][i:i + 1, :], (8, 128)) for b in range(i + 1)] for i in range(8)]
        rows = [jnp.broadcast_to(tiles[g][k:k + 1, :], (8, lanes)) for k in range(8)]
        for k in range(8):
            d = lax.rsqrt(piv[k][k])
            low = {i: piv[i][k] * d for i in range(k + 1, 8)}
            for i in range(k + 1, 8):
                for b in range(k + 1, i + 1):
                    piv[i][b] = piv[i][b] - low[i] * low[b]
            rows[k] = rows[k] * wide(d)
            for i in range(k + 1, 8):
                rows[i] = rows[i] - wide(low[i]) * rows[k]
            for t in range(g + 1, count):
                cols[t][k] = cols[t][k] * d
                for i in range(k + 1, 8):
                    cols[t][i] = cols[t][i] - low[i] * cols[t][k]
                tiles[t] = tiles[t] - wide(cols[t][k]) * rows[k]
        new = rows[0]
        for k in range(1, 8):
            new = jnp.where(sub == k, rows[k], new)
        tiles[g] = new
    w = jnp.concatenate(tiles, axis=0)
    return w[:, :n], w[:, n:]


def split(v):
    hi = v.astype(BF16)
    return hi, (v - hi.astype(F32)).astype(BF16)


def mm(a, b, dims):
    ah, al = split(a); bh, bl = split(b)
    dot = lambda p, q: lax.dot_general(p, q, (dims, ((), ())), preferred_element_type=F32)
    return dot(ah, bh) + (dot(ah, bl) + dot(al, bh))


def hi(a, b, dims):
    return lax.dot_general(a, b, (dims, ((), ())), precision=lax.Precision.HIGHEST, preferred_element_type=F32)


def factor_kernel(n, g_ref, r_ref, c_ref, c_out, l_out, d_out, w, low, dirs, sems):
    m = g_ref.shape[0]
    count = m // n
    pending = []

    def put(src, dst, k):
        copy = pltpu.make_async_copy(src, dst, sems.at[k])
        copy.start()
        pending.append(copy)

    put(c_ref, c_out, 0)
    w[...] = g_ref[...]
    r_io = lax.broadcasted_iota(jnp.int32, (n, n), 0)
    c_io = lax.broadcasted_iota(jnp.int32, (n, n), 1)
    xs, ups = [], []
    for k in range(count):
        s = slice(k * n, (k + 1) * n)
        u, v = eliminate(w[s, s], n)
        low[s, s] = jnp.where(r_io >= c_io, u.T, 0.0)
        if k + 1 < count:
            rest = slice((k + 1) * n, m)
            up = hi(v, w[s, rest], ((1,), (0,)))
            w[rest, rest] = w[rest, rest] - hi(up, up, ((0,), (0,)))
            low[rest, s] = up.T
            low[s, rest] = jnp.zeros((n, m - (k + 1) * n), F32)
            ups.append(up)
        put(low.at[s], l_out.at[s], 1 + k)
        acc = r_ref[s, :]
        for j in range(k):
            acc = acc - mm(ups[j][:, (k - j - 1) * n:(k - j) * n], xs[j], ((0,), (0,)))
        x = mm(v, acc, ((1,), (0,)))
        xs.append(x)
        dirs[s, :] = x.astype(BF16)
        put(dirs.at[s], d_out.at[s], 1 + count + k)
    for copy in pending:
        copy.wait()


def shards(sides, basis_cols, snapshots):
    ny, nz, nx, points = sides
    own_points = basis_cols.shape[0] // nx
    modes = basis_cols.shape[1]
    snaps = snapshots.shape[0]
    n = max(ny, nz)
    dma = pltpu.SemaphoreType.DMA
    chunk = HALF // n
    coefficients, gram, residual = pl.pallas_call(
        functools.partial(exchange, sides),
        out_shape=(
            jax.ShapeDtypeStruct((modes, snaps), F32),
            jax.ShapeDtypeStruct((snaps, snaps), F32),
            jax.ShapeDtypeStruct((snaps, own_points), F32),
        ),
        in_specs=[pl.BlockSpec(memory_space=pltpu.HBM)] * 2,
        out_specs=(pl.BlockSpec(memory_space=pltpu.VMEM),) * 3,
        scratch_shapes=[
            pltpu.VMEM(basis_cols.shape, BF16),
            pltpu.VMEM(snapshots.shape, BF16),
            pltpu.VMEM((nx, own_points, modes), BF16),
            pltpu.VMEM((nx, snaps, modes), BF16),
            pltpu.VMEM((snaps, modes), F32),
            pltpu.VMEM((snaps, modes), F32),
            pltpu.VMEM((snaps, snaps), F32),
            pltpu.VMEM((snaps, snaps), F32),
            pltpu.VMEM((2, HALF, snaps), F32),
            pltpu.VMEM((2, HALF, snaps), F32),
            pltpu.VMEM((2, n, chunk, snaps), F32),
            pltpu.VMEM((2, n, chunk, snaps), F32),
            pltpu.VMEM((nx, chunk, snaps), F32),
            dma((4,)),
            dma((nx,)), dma((nx,)),
            dma((2,)), dma((2,)),
            dma((2, n)), dma((2, n)),
            dma((2, n)), dma((2, n)),
            dma((2, nx)), dma((2, nx)),
            dma((2, n)), dma((2, n)),
            dma((2,)), dma((2,)),
            dma((n,)), dma((n,)),
            dma(()), dma(()),
        ],
        compiler_params=pltpu.CompilerParams(
            collective_id=0, has_side_effects=True, vmem_limit_bytes=52 << 20
        ),
        name="exchange",
    )(basis_cols, snapshots)
    block = 64
    coefficients, factor, directions = pl.pallas_call(
        functools.partial(factor_kernel, block),
        out_shape=(
            jax.ShapeDtypeStruct((modes, snaps), F32),
            jax.ShapeDtypeStruct((snaps, snaps), F32),
            jax.ShapeDtypeStruct((snaps, own_points), BF16),
        ),
        in_specs=[pl.BlockSpec(memory_space=pltpu.VMEM)] * 3,
        out_specs=(pl.BlockSpec(memory_space=pl.ANY),) * 3,
        scratch_shapes=[
            pltpu.VMEM((snaps, snaps), F32),
            pltpu.VMEM((snaps, snaps), F32),
            pltpu.VMEM((snaps, own_points), BF16),
            dma((1 + 2 * (snaps // block),)),
        ],
        compiler_params=pltpu.CompilerParams(vmem_limit_bytes=32 << 20),
        name="factor",
    )(gram, residual, coefficients)
    return (coefficients, factor, directions)


def solution(mesh):
    rows, cols = mesh.shape["rows"], mesh.shape["cols"]
    placed = (P("rows", "cols"), P(None, "rows"))

    def whole(basis_cols, snapshots):
        sides = (SIDE_Y, rows // (2 * SIDE_Y), cols, basis_cols.shape[0])
        return jax.shard_map(
            functools.partial(shards, sides),
            mesh=mesh,
            in_specs=placed,
            out_specs=(P("cols", None), P(), P(None, ("rows", "cols"))),
            check_vma=False,
        )(basis_cols, snapshots)

    return whole
```

```python
import functools
import math

import jax
import jax.numpy as jnp
from jax import lax
from jax.experimental import pallas as pl
from jax.experimental.pallas import tpu as pltpu
from jax.sharding import PartitionSpec as P

RANK = 1024
SIDE_Y = 8
MESH = pl.DeviceIdType.MESH
F32 = jnp.float32
BF16 = jnp.bfloat16
HALF = 128
SHARES = (7, 2, 4, 3)


def exchange(sides, b_hbm, s_hbm, coef_o, gram_o, res_o, bv, sv, bfull, qfull, cbuf, pbuf, pbuf2, gbuf,
             core_in, part, rs_in, ar_in, x_in, load_sem, bx_s, bx_r, core_s, core_r, rs_s, rs_r, ar_s, ar_r, x_s, x_r,
             ag_s, ag_r, out_s, out_r, cag_s, cag_r, cout_s, cout_r):
    ny, nz, nx, points = sides
    row, x = lax.axis_index("rows"), lax.axis_index("cols")
    z, y, c = row // (2 * ny), (row // 2) % ny, row % 2
    own_points = b_hbm.shape[0] // nx
    ring = ny
    rows = HALF // ring

    def device(z, y, c, x):
        return ((z * ny + y) * 2 + c, x)

    mate = device(z, y, 1 - c, x)
    far = sorted(range(1, ring), key=lambda k: -min(k, ring - k))
    one, two = jnp.where(c == 0, y, z), jnp.where(c == 0, z, y)
    one_peers = [lax.rem(one + k, ring) for k in far]
    two_peers = [lax.rem(two + k, ring) for k in far]
    x_peers = [lax.rem(x + k, nx) for k in sorted(range(1, nx), key=lambda k: -min(k, nx - k))]

    def along_one(t):
        return device(jnp.where(c == 0, z, t), jnp.where(c == 0, t, y), c, x)

    def along_two(t):
        return device(jnp.where(c == 0, t, z), jnp.where(c == 0, y, t), c, x)

    def along_x(t):
        return device(z, y, c, t)

    def remote(src, dst, send, recv, dev):
        return pltpu.make_async_remote_copy(
            src_ref=src, dst_ref=dst, send_sem=send, recv_sem=recv, device_id=dev, device_id_type=MESH
        )

    pending = []

    def send(*args):
        copy = remote(*args)
        copy.start()
        pending.append(copy)

    def arrived(ref, sem):
        remote(ref, ref, load_sem.at[3], sem, mate).wait_recv()

    load_b = pltpu.make_async_copy(b_hbm, bv, load_sem.at[0])
    load_s = pltpu.make_async_copy(s_hbm, sv, load_sem.at[1])
    load_b.start()
    load_s.start()

    barrier = pltpu.get_barrier_semaphore()
    peers = [mate] + [along_one(t) for t in one_peers] + [along_two(t) for t in two_peers]
    peers += [along_x(t) for t in x_peers]
    for peer in peers:
        pl.semaphore_signal(barrier, inc=1, device_id=peer, device_id_type=MESH)
    pl.semaphore_wait(barrier, len(peers))

    spans = [(sum(SHARES[:k]) * own_points // 16, SHARES[k] * own_points // 16) for k in range(len(SHARES))]

    def send_basis(k):
        start, size = spans[k]
        for t in x_peers:
            send(b_hbm.at[pl.ds(t * own_points + start, size)], bfull.at[x, pl.ds(start, size)], bx_s.at[k, t],
                 bx_r.at[k, x], along_x(t))

    send_basis(0)
    load_own = pltpu.make_async_copy(b_hbm.at[pl.ds(x * own_points, own_points)], bfull.at[x], load_sem.at[2])
    load_own.start()

    load_b.wait()
    load_s.wait()
    steps = 4
    depth = b_hbm.shape[0] // steps
    total = None
    for k in range(steps):
        piece = jnp.dot(sv[:, k * depth:(k + 1) * depth], bv[k * depth:(k + 1) * depth, :],
                        preferred_element_type=F32)
        total = piece if total is None else total + piece

    chunk = pl.ds(pl.multiple_of(one * rows, rows), rows)
    half = pl.ds(pl.multiple_of(c * HALF, HALF), HALF)
    other = pl.ds(pl.multiple_of((1 - c) * HALF, HALF), HALF)

    def half_chunk(t):
        return pl.ds(pl.multiple_of(c * HALF + t * rows, rows), rows)

    def row_sum(phase, buf, value):
        buf[...] = value
        send(buf.at[other], core_in.at[phase], core_s.at[phase], core_r.at[phase], mate)
        arrived(core_in.at[phase], core_r.at[phase])
        part[phase] = buf[half, :] + core_in[phase]
        for t in one_peers:
            send(part.at[phase, pl.ds(pl.multiple_of(t * rows, rows), rows)], rs_in.at[phase, one],
                 rs_s.at[phase, t], rs_r.at[phase, one], along_one(t))
        rs_in[phase, one] = part[phase, chunk, :]
        for t in one_peers:
            arrived(rs_in.at[phase, t], rs_r.at[phase, t])
        got = rs_in[phase, 0]
        for i in range(1, ring):
            got = got + rs_in[phase, i]
        ar_in[phase, two] = got
        for t in two_peers:
            send(ar_in.at[phase, two], ar_in.at[phase, two], ar_s.at[phase, t], ar_r.at[phase, two], along_two(t))
        for t in two_peers:
            arrived(ar_in.at[phase, t], ar_r.at[phase, t])
        got = ar_in[phase, 0]
        for i in range(1, ring):
            got = got + ar_in[phase, i]
        return got

    own = row_sum(0, pbuf, total) * (math.sqrt(RANK) / points)
    mine = half_chunk(one)
    qfull[x, mine, :] = own.astype(BF16)
    for t in x_peers:
        send(qfull.at[x, mine], qfull.at[x, mine], x_s.at[0, t], x_r.at[0, x], along_x(t))
    send_basis(1)
    cbuf[mine, :] = own
    for t in x_peers:
        arrived(qfull.at[t, mine], x_r.at[0, t])
    for t in one_peers:
        send(qfull.at[:, mine], qfull.at[:, mine], ag_s.at[0, t], ag_r.at[0, one], along_one(t))
    for t in one_peers:
        send(cbuf.at[mine], cbuf.at[mine], cag_s.at[t], cag_r.at[one], along_one(t))
    send_basis(2)
    for t in one_peers:
        arrived(qfull.at[:, half_chunk(t)], ag_r.at[0, t])
    send(qfull.at[:, half], qfull.at[:, half], out_s.at[0], out_r.at[0], mate)
    send_basis(3)
    arrived(qfull.at[:, other], out_r.at[0])

    def from_modes(t):
        return lax.dot_general(qfull[t], bfull[t], (((1,), (1,)), ((), ())), preferred_element_type=F32)

    load_own.wait()
    recon = from_modes(x)
    for t in reversed(x_peers):
        for k, (start, size) in enumerate(spans):
            arrived(bfull.at[t, pl.ds(start, size)], bx_r.at[k, t])
        recon = recon + from_modes(t)
    own_snaps = sv[:, pl.ds(pl.multiple_of(x * own_points, own_points), own_points)].astype(F32)
    residual = own_snaps - recon * (1.0 / math.sqrt(RANK))
    gram = lax.dot_general(residual, residual, (((1,), (1,)), ((), ())), precision=lax.Precision.HIGHEST,
                           preferred_element_type=F32) * (1.0 / points)
    res_o[...] = residual
    for t in one_peers:
        arrived(cbuf.at[half_chunk(t)], cag_r.at[t])
    send(cbuf.at[half], cbuf.at[half], cout_s, cout_r, mate)
    got = row_sum(1, pbuf2, gram)
    x_in[x] = got
    for t in x_peers:
        send(x_in.at[x], x_in.at[x], x_s.at[1, t], x_r.at[1, x], along_x(t))
    arrived(cbuf.at[other], cout_r)
    coef_o[...] = cbuf[...].T
    for t in x_peers:
        arrived(x_in.at[t], x_r.at[1, t])
    got = x_in[0]
    for i in range(1, nx):
        got = got + x_in[i]
    gbuf[mine, :] = got
    for t in one_peers:
        send(gbuf.at[mine], gbuf.at[mine], ag_s.at[1, t], ag_r.at[1, one], along_one(t))
    for t in one_peers:
        arrived(gbuf.at[half_chunk(t)], ag_r.at[1, t])
    send(gbuf.at[half], gbuf.at[half], out_s.at[1], out_r.at[1], mate)
    gram_o[half, :] = gbuf[half, :]
    arrived(gbuf.at[other], out_r.at[1])
    gram_o[other, :] = gbuf[other, :]
    for copy in pending:
        copy.wait_send()


def eliminate(a, n):
    lanes = 2 * n
    count = n // 8
    r_io = lax.broadcasted_iota(jnp.int32, (8, n), 0)
    c_io = lax.broadcasted_iota(jnp.int32, (8, n), 1)
    sub = lax.broadcasted_iota(jnp.int32, (8, lanes), 0)
    tiles = [jnp.concatenate([a[8 * t:8 * t + 8], jnp.where(c_io == r_io + 8 * t, 1.0, 0.0).astype(F32)], axis=1)
             for t in range(count)]
    def wide(v):
        return v if lanes == 128 else jnp.concatenate([v] * (lanes // 128), axis=1)
    for g in range(count):
        cols = {t: [jnp.broadcast_to(tiles[t][:, 8 * g + k:8 * g + k + 1], (8, 128)) for k in range(8)]
                for t in range(g, count)}
        piv = [[jnp.broadcast_to(cols[g][b][i:i + 1, :], (8, 128)) for b in range(i + 1)] for i in range(8)]
        rows = [jnp.broadcast_to(tiles[g][k:k + 1, :], (8, lanes)) for k in range(8)]
        for k in range(8):
            d = lax.rsqrt(piv[k][k])
            low = {i: piv[i][k] * d for i in range(k + 1, 8)}
            for i in range(k + 1, 8):
                for b in range(k + 1, i + 1):
                    piv[i][b] = piv[i][b] - low[i] * low[b]
            rows[k] = rows[k] * wide(d)
            for i in range(k + 1, 8):
                rows[i] = rows[i] - wide(low[i]) * rows[k]
            for t in range(g + 1, count):
                cols[t][k] = cols[t][k] * d
                for i in range(k + 1, 8):
                    cols[t][i] = cols[t][i] - low[i] * cols[t][k]
                tiles[t] = tiles[t] - wide(cols[t][k]) * rows[k]
        new = rows[0]
        for k in range(1, 8):
            new = jnp.where(sub == k, rows[k], new)
        tiles[g] = new
    w = jnp.concatenate(tiles, axis=0)
    return w[:, :n], w[:, n:]


def split(v):
    hi = v.astype(BF16)
    return hi, (v - hi.astype(F32)).astype(BF16)


def mm(a, b, dims):
    ah, al = split(a); bh, bl = split(b)
    dot = lambda p, q: lax.dot_general(p, q, (dims, ((), ())), preferred_element_type=F32)
    return dot(ah, bh) + (dot(ah, bl) + dot(al, bh))


def hi(a, b, dims):
    return lax.dot_general(a, b, (dims, ((), ())), precision=lax.Precision.HIGHEST, preferred_element_type=F32)


def factor_kernel(n, g_ref, r_ref, c_ref, c_out, l_out, d_out, w, low, dirs, sems):
    m = g_ref.shape[0]
    count = m // n
    pending = []

    def put(src, dst, k):
        copy = pltpu.make_async_copy(src, dst, sems.at[k])
        copy.start()
        pending.append(copy)

    put(c_ref, c_out, 0)
    w[...] = g_ref[...]
    r_io = lax.broadcasted_iota(jnp.int32, (n, n), 0)
    c_io = lax.broadcasted_iota(jnp.int32, (n, n), 1)
    xs, ups = [], []
    for k in range(count):
        s = slice(k * n, (k + 1) * n)
        u, v = eliminate(w[s, s], n)
        low[s, s] = jnp.where(r_io >= c_io, u.T, 0.0)
        if k + 1 < count:
            rest = slice((k + 1) * n, m)
            up = hi(v, w[s, rest], ((1,), (0,)))
            w[rest, rest] = w[rest, rest] - hi(up, up, ((0,), (0,)))
            low[rest, s] = up.T
            low[s, rest] = jnp.zeros((n, m - (k + 1) * n), F32)
            ups.append(up)
        put(low.at[s], l_out.at[s], 1 + k)
        acc = r_ref[s, :]
        for j in range(k):
            acc = acc - mm(ups[j][:, (k - j - 1) * n:(k - j) * n], xs[j], ((0,), (0,)))
        x = mm(v, acc, ((1,), (0,)))
        xs.append(x)
        dirs[s, :] = x.astype(BF16)
        put(dirs.at[s], d_out.at[s], 1 + count + k)
    for copy in pending:
        copy.wait()


def shards(sides, basis_cols, snapshots):
    ny, nz, nx, points = sides
    own_points = basis_cols.shape[0] // nx
    modes = basis_cols.shape[1]
    snaps = snapshots.shape[0]
    n = max(ny, nz)
    dma = pltpu.SemaphoreType.DMA
    chunk = HALF // n
    coefficients, gram, residual = pl.pallas_call(
        functools.partial(exchange, sides),
        out_shape=(
            jax.ShapeDtypeStruct((modes, snaps), F32),
            jax.ShapeDtypeStruct((snaps, snaps), F32),
            jax.ShapeDtypeStruct((snaps, own_points), F32),
        ),
        in_specs=[pl.BlockSpec(memory_space=pltpu.HBM)] * 2,
        out_specs=(pl.BlockSpec(memory_space=pltpu.VMEM),) * 3,
        scratch_shapes=[
            pltpu.VMEM(basis_cols.shape, BF16),
            pltpu.VMEM(snapshots.shape, BF16),
            pltpu.VMEM((nx, own_points, modes), BF16),
            pltpu.VMEM((nx, snaps, modes), BF16),
            pltpu.VMEM((snaps, modes), F32),
            pltpu.VMEM((snaps, modes), F32),
            pltpu.VMEM((snaps, snaps), F32),
            pltpu.VMEM((snaps, snaps), F32),
            pltpu.VMEM((2, HALF, snaps), F32),
            pltpu.VMEM((2, HALF, snaps), F32),
            pltpu.VMEM((2, n, chunk, snaps), F32),
            pltpu.VMEM((2, n, chunk, snaps), F32),
            pltpu.VMEM((nx, chunk, snaps), F32),
            dma((4,)),
            dma((len(SHARES), nx)), dma((len(SHARES), nx)),
            dma((2,)), dma((2,)),
            dma((2, n)), dma((2, n)),
            dma((2, n)), dma((2, n)),
            dma((2, nx)), dma((2, nx)),
            dma((2, n)), dma((2, n)),
            dma((2,)), dma((2,)),
            dma((n,)), dma((n,)),
            dma(()), dma(()),
        ],
        compiler_params=pltpu.CompilerParams(
            collective_id=0, has_side_effects=True, vmem_limit_bytes=52 << 20
        ),
        name="exchange",
    )(basis_cols, snapshots)
    block = 64
    coefficients, factor, directions = pl.pallas_call(
        functools.partial(factor_kernel, block),
        out_shape=(
            jax.ShapeDtypeStruct((modes, snaps), F32),
            jax.ShapeDtypeStruct((snaps, snaps), F32),
            jax.ShapeDtypeStruct((snaps, own_points), BF16),
        ),
        in_specs=[pl.BlockSpec(memory_space=pltpu.VMEM)] * 3,
        out_specs=(pl.BlockSpec(memory_space=pl.ANY),) * 3,
        scratch_shapes=[
            pltpu.VMEM((snaps, snaps), F32),
            pltpu.VMEM((snaps, snaps), F32),
            pltpu.VMEM((snaps, own_points), BF16),
            dma((1 + 2 * (snaps // block),)),
        ],
        compiler_params=pltpu.CompilerParams(vmem_limit_bytes=32 << 20),
        name="factor",
    )(gram, residual, coefficients)
    return (coefficients, factor, directions)


def solution(mesh):
    rows, cols = mesh.shape["rows"], mesh.shape["cols"]
    placed = (P("rows", "cols"), P(None, "rows"))

    def whole(basis_cols, snapshots):
        sides = (SIDE_Y, rows // (2 * SIDE_Y), cols, basis_cols.shape[0])
        return jax.shard_map(
            functools.partial(shards, sides),
            mesh=mesh,
            in_specs=placed,
            out_specs=(P("cols", None), P(), P(None, ("rows", "cols"))),
            check_vma=False,
        )(basis_cols, snapshots)

    return whole
```

```python
import functools
import math

import jax
import jax.numpy as jnp
from jax import lax
from jax.experimental import pallas as pl
from jax.experimental.pallas import tpu as pltpu
from jax.sharding import PartitionSpec as P

RANK = 1024
SIDE_Y = 8
MESH = pl.DeviceIdType.MESH
F32 = jnp.float32
BF16 = jnp.bfloat16
HALF = 128
SHARES = (7, 2, 4, 3)


def exchange(sides, b_hbm, s_hbm, coef_o, gram_o, res_o, bv, sv, bfull, qfull, cbuf, pbuf, pbuf2, gbuf,
             core_in, part, rs_in, ar_in, x_in, load_sem, bx_s, bx_r, core_s, core_r, rs_s, rs_r, ar_s, ar_r, x_s, x_r,
             ag_s, ag_r, out_s, out_r, cag_s, cag_r, cout_s, cout_r):
    ny, nz, nx, points = sides
    row, x = lax.axis_index("rows"), lax.axis_index("cols")
    z, y, c = row // (2 * ny), (row // 2) % ny, row % 2
    own_points = b_hbm.shape[0] // nx
    ring = ny
    rows = HALF // ring

    def device(z, y, c, x):
        return ((z * ny + y) * 2 + c, x)

    mate = device(z, y, 1 - c, x)
    far = sorted(range(1, ring), key=lambda k: -min(k, ring - k))
    one, two = jnp.where(c == 0, y, z), jnp.where(c == 0, z, y)
    one_peers = [lax.rem(one + k, ring) for k in far]
    two_peers = [lax.rem(two + k, ring) for k in far]
    x_peers = [lax.rem(x + k, nx) for k in sorted(range(1, nx), key=lambda k: -min(k, nx - k))]

    def along_one(t):
        return device(jnp.where(c == 0, z, t), jnp.where(c == 0, t, y), c, x)

    def along_two(t):
        return device(jnp.where(c == 0, t, z), jnp.where(c == 0, y, t), c, x)

    def along_x(t):
        return device(z, y, c, t)

    def remote(src, dst, send, recv, dev):
        return pltpu.make_async_remote_copy(
            src_ref=src, dst_ref=dst, send_sem=send, recv_sem=recv, device_id=dev, device_id_type=MESH
        )

    pending = []

    def send(*args):
        copy = remote(*args)
        copy.start()
        pending.append(copy)

    def arrived(ref, sem):
        remote(ref, ref, load_sem.at[3], sem, mate).wait_recv()

    load_b = pltpu.make_async_copy(b_hbm, bv, load_sem.at[0])
    load_s = pltpu.make_async_copy(s_hbm, sv, load_sem.at[1])
    load_b.start()
    load_s.start()

    barrier = pltpu.get_barrier_semaphore()
    peers = [mate] + [along_one(t) for t in one_peers] + [along_two(t) for t in two_peers]
    peers += [along_x(t) for t in x_peers]
    for peer in peers:
        pl.semaphore_signal(barrier, inc=1, device_id=peer, device_id_type=MESH)
    pl.semaphore_wait(barrier, len(peers))

    spans = [(sum(SHARES[:k]) * own_points // 16, SHARES[k] * own_points // 16) for k in range(len(SHARES))]

    def send_basis(k):
        start, size = spans[k]
        for t in x_peers:
            send(b_hbm.at[pl.ds(t * own_points + start, size)], bfull.at[x, pl.ds(start, size)], bx_s.at[k, t],
                 bx_r.at[k, x], along_x(t))

    send_basis(0)
    load_own = pltpu.make_async_copy(b_hbm.at[pl.ds(x * own_points, own_points)], bfull.at[x], load_sem.at[2])
    load_own.start()

    load_b.wait()
    load_s.wait()
    steps = 4
    depth = b_hbm.shape[0] // steps
    total = None
    for k in range(steps):
        piece = jnp.dot(sv[:, k * depth:(k + 1) * depth], bv[k * depth:(k + 1) * depth, :],
                        preferred_element_type=F32)
        total = piece if total is None else total + piece

    chunk = pl.ds(pl.multiple_of(one * rows, rows), rows)
    half = pl.ds(pl.multiple_of(c * HALF, HALF), HALF)
    other = pl.ds(pl.multiple_of((1 - c) * HALF, HALF), HALF)

    def half_chunk(t):
        return pl.ds(pl.multiple_of(c * HALF + t * rows, rows), rows)

    def row_sum(phase, buf, value):
        buf[...] = value
        send(buf.at[other], core_in.at[phase], core_s.at[phase], core_r.at[phase], mate)
        arrived(core_in.at[phase], core_r.at[phase])
        part[phase] = buf[half, :] + core_in[phase]
        for t in one_peers:
            send(part.at[phase, pl.ds(pl.multiple_of(t * rows, rows), rows)], rs_in.at[phase, one],
                 rs_s.at[phase, t], rs_r.at[phase, one], along_one(t))
        rs_in[phase, one] = part[phase, chunk, :]
        for t in one_peers:
            arrived(rs_in.at[phase, t], rs_r.at[phase, t])
        got = rs_in[phase, 0]
        for i in range(1, ring):
            got = got + rs_in[phase, i]
        ar_in[phase, two] = got
        for t in two_peers:
            send(ar_in.at[phase, two], ar_in.at[phase, two], ar_s.at[phase, t], ar_r.at[phase, two], along_two(t))
        for t in two_peers:
            arrived(ar_in.at[phase, t], ar_r.at[phase, t])
        got = ar_in[phase, 0]
        for i in range(1, ring):
            got = got + ar_in[phase, i]
        return got

    own = row_sum(0, pbuf, total) * (math.sqrt(RANK) / points)
    mine = half_chunk(one)
    qfull[x, mine, :] = own.astype(BF16)
    for t in x_peers:
        send(qfull.at[x, mine], qfull.at[x, mine], x_s.at[0, t], x_r.at[0, x], along_x(t))
    send_basis(1)
    cbuf[mine, :] = own
    for t in x_peers:
        arrived(qfull.at[t, mine], x_r.at[0, t])
    for t in one_peers:
        send(qfull.at[:, mine], qfull.at[:, mine], ag_s.at[0, t], ag_r.at[0, one], along_one(t))
    for t in one_peers:
        send(cbuf.at[mine], cbuf.at[mine], cag_s.at[t], cag_r.at[one], along_one(t))
    send_basis(2)
    for t in one_peers:
        arrived(qfull.at[:, half_chunk(t)], ag_r.at[0, t])
    send(qfull.at[:, half], qfull.at[:, half], out_s.at[0], out_r.at[0], mate)
    send_basis(3)
    arrived(qfull.at[:, other], out_r.at[0])

    def from_modes(t):
        return lax.dot_general(qfull[t], bfull[t], (((1,), (1,)), ((), ())), preferred_element_type=F32)

    load_own.wait()
    recon = from_modes(x)
    for t in reversed(x_peers):
        for k, (start, size) in enumerate(spans):
            arrived(bfull.at[t, pl.ds(start, size)], bx_r.at[k, t])
        recon = recon + from_modes(t)
    own_snaps = sv[:, pl.ds(pl.multiple_of(x * own_points, own_points), own_points)].astype(F32)
    residual = own_snaps - recon * (1.0 / math.sqrt(RANK))
    gram = lax.dot_general(residual, residual, (((1,), (1,)), ((), ())), precision=lax.Precision.HIGHEST,
                           preferred_element_type=F32) * (1.0 / points)
    res_o[...] = residual
    for t in one_peers:
        arrived(cbuf.at[half_chunk(t)], cag_r.at[t])
    send(cbuf.at[half], cbuf.at[half], cout_s, cout_r, mate)
    got = row_sum(1, pbuf2, gram)
    x_in[x] = got
    for t in x_peers:
        send(x_in.at[x], x_in.at[x], x_s.at[1, t], x_r.at[1, x], along_x(t))
    arrived(cbuf.at[other], cout_r)
    coef_o[...] = cbuf[...].T
    for t in x_peers:
        arrived(x_in.at[t], x_r.at[1, t])
    got = x_in[0]
    for i in range(1, nx):
        got = got + x_in[i]
    gbuf[mine, :] = got
    for t in one_peers:
        send(gbuf.at[mine], gbuf.at[mine], ag_s.at[1, t], ag_r.at[1, one], along_one(t))
    for t in one_peers:
        arrived(gbuf.at[half_chunk(t)], ag_r.at[1, t])
    send(gbuf.at[half], gbuf.at[half], out_s.at[1], out_r.at[1], mate)
    gram_o[half, :] = gbuf[half, :]
    arrived(gbuf.at[other], out_r.at[1])
    gram_o[other, :] = gbuf[other, :]
    for copy in pending:
        copy.wait_send()


def eliminate(a, n, buf):
    lanes = 2 * n
    count = n // 8
    r_io = lax.broadcasted_iota(jnp.int32, (8, n), 0)
    c_io = lax.broadcasted_iota(jnp.int32, (8, n), 1)
    sub = lax.broadcasted_iota(jnp.int32, (8, lanes), 0)
    tiles = [jnp.concatenate([jnp.where(c_io == r_io + 8 * t, 1.0, 0.0).astype(F32), a[8 * t:8 * t + 8]], axis=1)
             for t in range(count)]

    def spread(v):
        return jnp.broadcast_to(v, (8, lanes))

    for g in range(count):
        base, slot = n + 8 * g, g % 2
        cols = {t: [spread(tiles[t][:, base + k:base + k + 1]) for k in range(8)] for t in range(g, count)}
        for k in range(8):
            buf[slot, k] = cols[g][k]
        buf[slot, 8] = tiles[g]
        piv = [[spread(buf[slot, b, i:i + 1, :]) for b in range(i + 1)] for i in range(8)]
        rows = [spread(buf[slot, 8, k:k + 1, :]) for k in range(8)]
        for k in range(8):
            d = lax.rsqrt(piv[k][k])
            inv = pl.reciprocal(piv[k][k], approx=True)
            for i in range(k + 1, 8):
                for b in range(k + 1, i + 1):
                    piv[i][b] = piv[i][b] - (piv[i][k] * piv[b][k]) * inv
            low = {i: piv[i][k] * d for i in range(k + 1, 8)}
            rows[k] = rows[k] * d
            for i in range(k + 1, 8):
                rows[i] = rows[i] - low[i] * rows[k]
            for t in range(g + 1, count):
                cols[t][k] = cols[t][k] * d
                for i in range(k + 1, 8):
                    cols[t][i] = cols[t][i] - low[i] * cols[t][k]
                tiles[t] = tiles[t] - cols[t][k] * rows[k]
        new = rows[0]
        for k in range(1, 8):
            new = jnp.where(sub == k, rows[k], new)
        tiles[g] = new
    w = jnp.concatenate(tiles, axis=0)
    return w[:, :n], w[:, n:]


NN, NT = ((1,), (0,)), ((1,), (1,))


def split(v):
    high = v.astype(BF16)
    return high, (v - high.astype(F32)).astype(BF16)


def three(a, b, dims):
    (ah, al), (bh, bl) = split(a), split(b)

    def dot(p, q):
        return lax.dot_general(p, q, (dims, ((), ())), preferred_element_type=F32)

    return dot(ah, bh) + (dot(ah, bl) + dot(al, bh))


def full(a, b, dims):
    return lax.dot_general(a, b, (dims, ((), ())), precision=lax.Precision.HIGHEST, preferred_element_type=F32)


def factor_kernel(n, g_ref, r_ref, c_ref, c_out, l_out, d_out, factor, dirs, buf, sems):
    count = g_ref.shape[0] // n
    pending = []

    def put(src, dst, k):
        copy = pltpu.make_async_copy(src, dst, sems.at[k])
        copy.start()
        pending.append(copy)

    def span(k):
        return slice(k * n, (k + 1) * n)

    put(c_ref, c_out, 0)
    r_io = lax.broadcasted_iota(jnp.int32, (n, n), 0)
    c_io = lax.broadcasted_iota(jnp.int32, (n, n), 1)
    block = {(i, k): g_ref[span(i), span(k)] for k in range(count) for i in range(k, count)}
    low, xs = {}, []
    for k in range(count):
        v, u = eliminate(block[k, k], n, buf)
        factor[span(k), span(k)] = jnp.where(r_io >= c_io, u.T, 0.0)
        for i in range(k + 1, count):
            low[i, k] = full(block[i, k], v, NT)
            factor[span(i), span(k)] = low[i, k]
            factor[span(k), span(i)] = jnp.zeros((n, n), F32)
            if i == k + 1:
                block[i, i] = block[i, i] - full(low[i, k], low[i, k], NT)
        for i in range(k + 2, count):
            for j in range(k + 1, i + 1):
                block[i, j] = block[i, j] - full(low[i, k], low[j, k], NT)
        put(factor.at[span(k)], l_out.at[span(k)], 1 + k)
        acc = r_ref[span(k), :]
        for j in range(k):
            acc = acc - three(low[k, j], xs[j], NN)
        xs.append(three(v, acc, NN))
        dirs[span(k), :] = xs[k].astype(BF16)
        put(dirs.at[span(k)], d_out.at[span(k)], 1 + count + k)
    for copy in pending:
        copy.wait()


def shards(sides, basis_cols, snapshots):
    ny, nz, nx, points = sides
    own_points = basis_cols.shape[0] // nx
    modes = basis_cols.shape[1]
    snaps = snapshots.shape[0]
    n = max(ny, nz)
    dma = pltpu.SemaphoreType.DMA
    chunk = HALF // n
    coefficients, gram, residual = pl.pallas_call(
        functools.partial(exchange, sides),
        out_shape=(
            jax.ShapeDtypeStruct((modes, snaps), F32),
            jax.ShapeDtypeStruct((snaps, snaps), F32),
            jax.ShapeDtypeStruct((snaps, own_points), F32),
        ),
        in_specs=[pl.BlockSpec(memory_space=pltpu.HBM)] * 2,
        out_specs=(pl.BlockSpec(memory_space=pltpu.VMEM),) * 3,
        scratch_shapes=[
            pltpu.VMEM(basis_cols.shape, BF16),
            pltpu.VMEM(snapshots.shape, BF16),
            pltpu.VMEM((nx, own_points, modes), BF16),
            pltpu.VMEM((nx, snaps, modes), BF16),
            pltpu.VMEM((snaps, modes), F32),
            pltpu.VMEM((snaps, modes), F32),
            pltpu.VMEM((snaps, snaps), F32),
            pltpu.VMEM((snaps, snaps), F32),
            pltpu.VMEM((2, HALF, snaps), F32),
            pltpu.VMEM((2, HALF, snaps), F32),
            pltpu.VMEM((2, n, chunk, snaps), F32),
            pltpu.VMEM((2, n, chunk, snaps), F32),
            pltpu.VMEM((nx, chunk, snaps), F32),
            dma((4,)),
            dma((len(SHARES), nx)), dma((len(SHARES), nx)),
            dma((2,)), dma((2,)),
            dma((2, n)), dma((2, n)),
            dma((2, n)), dma((2, n)),
            dma((2, nx)), dma((2, nx)),
            dma((2, n)), dma((2, n)),
            dma((2,)), dma((2,)),
            dma((n,)), dma((n,)),
            dma(()), dma(()),
        ],
        compiler_params=pltpu.CompilerParams(
            collective_id=0, has_side_effects=True, vmem_limit_bytes=52 << 20
        ),
        name="exchange",
    )(basis_cols, snapshots)
    block = 64
    coefficients, factor, directions = pl.pallas_call(
        functools.partial(factor_kernel, block),
        out_shape=(
            jax.ShapeDtypeStruct((modes, snaps), F32),
            jax.ShapeDtypeStruct((snaps, snaps), F32),
            jax.ShapeDtypeStruct((snaps, own_points), BF16),
        ),
        in_specs=[pl.BlockSpec(memory_space=pltpu.VMEM)] * 3,
        out_specs=(pl.BlockSpec(memory_space=pl.ANY),) * 3,
        scratch_shapes=[
            pltpu.VMEM((snaps, snaps), F32),
            pltpu.VMEM((snaps, own_points), BF16),
            pltpu.VMEM((2, 9, 8, 2 * block), F32),
            dma((1 + 2 * (snaps // block),)),
        ],
        compiler_params=pltpu.CompilerParams(vmem_limit_bytes=32 << 20),
        name="factor",
    )(gram, residual, coefficients)
    return (coefficients, factor, directions)


def solution(mesh):
    rows, cols = mesh.shape["rows"], mesh.shape["cols"]
    placed = (P("rows", "cols"), P(None, "rows"))

    def whole(basis_cols, snapshots):
        sides = (SIDE_Y, rows // (2 * SIDE_Y), cols, basis_cols.shape[0])
        return jax.shard_map(
            functools.partial(shards, sides),
            mesh=mesh,
            in_specs=placed,
            out_specs=(P("cols", None), P(), P(None, ("rows", "cols"))),
            check_vma=False,
        )(basis_cols, snapshots)

    return whole
```

```python
import functools
import math

import jax
import jax.numpy as jnp
from jax import lax
from jax.experimental import pallas as pl
from jax.experimental.pallas import tpu as pltpu
from jax.sharding import PartitionSpec as P

RANK = 1024
SIDE_Y = 8
MESH = pl.DeviceIdType.MESH
F32 = jnp.float32
BF16 = jnp.bfloat16
HALF = 128
SHARES = (7, 2, 4, 3)


def exchange(sides, b_hbm, s_hbm, coef_o, gram_o, res_o, bv, sv, bfull, qfull, cbuf, pbuf, psum,
             p_core, p_rs, p_ar, gbuf, gsum, g_core, g_rs, g_ar, x_in, gall, load_sem, bx_s, bx_r, core_s, core_r, rs_s, rs_r, ar_s, ar_r, x_s, x_r,
             ag_s, ag_r, out_s, out_r, cag_s, cag_r, cout_s, cout_r):
    ny, nz, nx, points = sides
    row, x = lax.axis_index("rows"), lax.axis_index("cols")
    z, y, c = row // (2 * ny), (row // 2) % ny, row % 2
    own_points = b_hbm.shape[0] // nx
    ring = ny
    rows = HALF // ring

    def device(z, y, c, x):
        return ((z * ny + y) * 2 + c, x)

    mate = device(z, y, 1 - c, x)
    far = sorted(range(1, ring), key=lambda k: -min(k, ring - k))
    one, two = jnp.where(c == 0, y, z), jnp.where(c == 0, z, y)
    one_peers = [lax.rem(one + k, ring) for k in far]
    two_peers = [lax.rem(two + k, ring) for k in far]
    x_peers = [lax.rem(x + k, nx) for k in sorted(range(1, nx), key=lambda k: -min(k, nx - k))]

    def along_one(t):
        return device(jnp.where(c == 0, z, t), jnp.where(c == 0, t, y), c, x)

    def along_two(t):
        return device(jnp.where(c == 0, t, z), jnp.where(c == 0, y, t), c, x)

    def along_x(t):
        return device(z, y, c, t)

    def remote(src, dst, send, recv, dev):
        return pltpu.make_async_remote_copy(
            src_ref=src, dst_ref=dst, send_sem=send, recv_sem=recv, device_id=dev, device_id_type=MESH
        )

    pending = []

    def send(*args):
        copy = remote(*args)
        copy.start()
        pending.append(copy)

    def arrived(ref, sem):
        remote(ref, ref, load_sem.at[3], sem, mate).wait_recv()

    load_b = pltpu.make_async_copy(b_hbm, bv, load_sem.at[0])
    load_s = pltpu.make_async_copy(s_hbm, sv, load_sem.at[1])
    load_b.start()
    load_s.start()

    barrier = pltpu.get_barrier_semaphore()
    peers = [mate] + [along_one(t) for t in one_peers] + [along_two(t) for t in two_peers]
    peers += [along_x(t) for t in x_peers]
    for peer in peers:
        pl.semaphore_signal(barrier, inc=1, device_id=peer, device_id_type=MESH)
    pl.semaphore_wait(barrier, len(peers))

    spans = [(sum(SHARES[:k]) * own_points // 16, SHARES[k] * own_points // 16) for k in range(len(SHARES))]

    def send_basis(k):
        start, size = spans[k]
        for t in x_peers:
            send(b_hbm.at[pl.ds(t * own_points + start, size)], bfull.at[x, pl.ds(start, size)], bx_s.at[k, t],
                 bx_r.at[k, x], along_x(t))

    send_basis(0)
    load_own = pltpu.make_async_copy(b_hbm.at[pl.ds(x * own_points, own_points)], bfull.at[x], load_sem.at[2])
    load_own.start()

    load_b.wait()
    load_s.wait()
    steps = 4
    depth = b_hbm.shape[0] // steps
    total = None
    for k in range(steps):
        piece = jnp.dot(sv[:, k * depth:(k + 1) * depth], bv[k * depth:(k + 1) * depth, :],
                        preferred_element_type=F32)
        total = piece if total is None else total + piece

    half = pl.ds(pl.multiple_of(c * HALF, HALF), HALF)
    other = pl.ds(pl.multiple_of((1 - c) * HALF, HALF), HALF)

    def half_chunk(t):
        return pl.ds(pl.multiple_of(c * HALF + t * rows, rows), rows)

    def row_sum(phase, own_sum, buf, core_in, rs_in, ar_in):
        send(buf.at[1 - c], core_in, core_s.at[phase], core_r.at[phase], mate)
        arrived(core_in, core_r.at[phase])
        own_sum[...] = buf[c] + core_in[...]
        size = own_sum.shape[0] // ring

        def piece(t):
            return pl.ds(pl.multiple_of(t * size, size), size)

        for t in one_peers:
            send(own_sum.at[piece(t)], rs_in.at[one], rs_s.at[phase, t], rs_r.at[phase, one], along_one(t))
        rs_in[one] = own_sum[piece(one), :]
        for t in one_peers:
            arrived(rs_in.at[t], rs_r.at[phase, t])
        got = rs_in[0]
        for i in range(1, ring):
            got = got + rs_in[i]
        ar_in[two] = got
        for t in two_peers:
            send(ar_in.at[two], ar_in.at[two], ar_s.at[phase, t], ar_r.at[phase, two], along_two(t))
        for t in two_peers:
            arrived(ar_in.at[t], ar_r.at[phase, t])
        got = ar_in[0]
        for i in range(1, ring):
            got = got + ar_in[i]
        return got

    pbuf[0], pbuf[1] = total[:HALF], total[HALF:]
    own = row_sum(0, psum, pbuf, p_core, p_rs, p_ar) * (math.sqrt(RANK) / points)
    mine = half_chunk(one)
    qfull[x, mine, :] = own.astype(BF16)
    for t in x_peers:
        send(qfull.at[x, mine], qfull.at[x, mine], x_s.at[0, t], x_r.at[0, x], along_x(t))
    send_basis(1)
    cbuf[mine, :] = own
    for t in x_peers:
        arrived(qfull.at[t, mine], x_r.at[0, t])
    for t in one_peers:
        send(qfull.at[:, mine], qfull.at[:, mine], ag_s.at[0, t], ag_r.at[0, one], along_one(t))
    for t in one_peers:
        send(cbuf.at[mine], cbuf.at[mine], cag_s.at[t], cag_r.at[one], along_one(t))
    send_basis(2)
    for t in one_peers:
        arrived(qfull.at[:, half_chunk(t)], ag_r.at[0, t])
    send(qfull.at[:, half], qfull.at[:, half], out_s.at[0], out_r.at[0], mate)
    send_basis(3)
    arrived(qfull.at[:, other], out_r.at[0])

    for t in one_peers:
        arrived(cbuf.at[half_chunk(t)], cag_r.at[t])
    send(cbuf.at[half], cbuf.at[half], cout_s, cout_r, mate)

    def sent():
        while pending:
            pending.pop().wait_send()

    def from_modes(t):
        return lax.dot_general(qfull[t], bfull[t], (((1,), (1,)), ((), ())), preferred_element_type=F32)

    load_own.wait()
    recon = from_modes(x)
    for t in reversed(x_peers):
        for k, (start, size) in enumerate(spans):
            arrived(bfull.at[t, pl.ds(start, size)], bx_r.at[k, t])
        recon = recon + from_modes(t)
    own_snaps = sv[:, pl.ds(pl.multiple_of(x * own_points, own_points), own_points)].astype(F32)
    residual = own_snaps - recon * (1.0 / math.sqrt(RANK))
    gram = lax.dot_general(residual, residual, (((1,), (1,)), ((), ())), precision=lax.Precision.HIGHEST,
                           preferred_element_type=F32) * (1.0 / points)
    res_o[...] = residual
    q = HALF // 2
    for h, (top, low) in enumerate(((0, 3 * q), (q, HALF))):
        gbuf[h, :, :HALF] = gram[top:top + q, :HALF]
        gbuf[h, :, HALF:] = gram[low:low + q, :]
    got = row_sum(1, gsum, gbuf, g_core, g_rs, g_ar)
    x_in[x] = got
    for t in x_peers:
        send(x_in.at[x], x_in.at[x], x_s.at[1, t], x_r.at[1, x], along_x(t))
    arrived(cbuf.at[other], cout_r)
    coef_o[...] = cbuf[...].T
    sent()
    for t in x_peers:
        arrived(x_in.at[t], x_r.at[1, t])
    got = x_in[0]
    for i in range(1, nx):
        got = got + x_in[i]
    size = q // ring

    def gram_rows(t):
        return gall.at[c, pl.ds(pl.multiple_of(t * size, size), size)]

    gall[c, pl.ds(pl.multiple_of(one * size, size), size), :] = got
    for t in one_peers:
        send(gram_rows(one), gram_rows(one), ag_s.at[1, t], ag_r.at[1, one], along_one(t))
    for t in one_peers:
        arrived(gram_rows(t), ag_r.at[1, t])
    send(gall.at[c], gall.at[c], out_s.at[1], out_r.at[1], mate)
    gram_o[c] = gall[c]
    sent()
    arrived(gall.at[1 - c], out_r.at[1])
    gram_o[1 - c] = gall[1 - c]


def eliminate(a, n, buf):
    lanes = 2 * n
    count = n // 8
    r_io = lax.broadcasted_iota(jnp.int32, (8, n), 0)
    c_io = lax.broadcasted_iota(jnp.int32, (8, n), 1)
    sub = lax.broadcasted_iota(jnp.int32, (8, lanes), 0)
    tiles = [jnp.concatenate([jnp.where(c_io == r_io + 8 * t, 1.0, 0.0).astype(F32), a[8 * t:8 * t + 8]], axis=1)
             for t in range(count)]

    def spread(v):
        return jnp.broadcast_to(v, (8, lanes))

    for g in range(count):
        base, slot = n + 8 * g, g % 2
        cols = {t: [spread(tiles[t][:, base + k:base + k + 1]) for k in range(8)] for t in range(g, count)}
        for k in range(8):
            buf[slot, k] = cols[g][k]
        buf[slot, 8] = tiles[g]
        piv = [[spread(buf[slot, b, i:i + 1, :]) for b in range(i + 1)] for i in range(8)]
        rows = [spread(buf[slot, 8, k:k + 1, :]) for k in range(8)]
        for k in range(8):
            d = lax.rsqrt(piv[k][k])
            inv = pl.reciprocal(piv[k][k], approx=True)
            for i in range(k + 1, 8):
                for b in range(k + 1, i + 1):
                    piv[i][b] = piv[i][b] - (piv[i][k] * piv[b][k]) * inv
            low = {i: piv[i][k] * d for i in range(k + 1, 8)}
            rows[k] = rows[k] * d
            for i in range(k + 1, 8):
                rows[i] = rows[i] - low[i] * rows[k]
            for t in range(g + 1, count):
                cols[t][k] = cols[t][k] * d
                for i in range(k + 1, 8):
                    cols[t][i] = cols[t][i] - low[i] * cols[t][k]
                tiles[t] = tiles[t] - cols[t][k] * rows[k]
        new = rows[0]
        for k in range(1, 8):
            new = jnp.where(sub == k, rows[k], new)
        tiles[g] = new
    w = jnp.concatenate(tiles, axis=0)
    return w[:, :n], w[:, n:]


NN, NT = ((1,), (0,)), ((1,), (1,))


def split(v):
    high = v.astype(BF16)
    return high, (v - high.astype(F32)).astype(BF16)


def three(a, b, dims):
    (ah, al), (bh, bl) = split(a), split(b)

    def dot(p, q):
        return lax.dot_general(p, q, (dims, ((), ())), preferred_element_type=F32)

    return dot(ah, bh) + (dot(ah, bl) + dot(al, bh))


def full(a, b, dims):
    return lax.dot_general(a, b, (dims, ((), ())), precision=lax.Precision.HIGHEST, preferred_element_type=F32)


def factor_kernel(n, g_ref, r_ref, c_ref, c_out, l_out, d_out, factor, dirs, buf, sems):
    count = r_ref.shape[0] // n
    pending = []

    def put(src, dst, k):
        copy = pltpu.make_async_copy(src, dst, sems.at[k])
        copy.start()
        pending.append(copy)

    def span(k):
        return slice(k * n, (k + 1) * n)

    put(c_ref, c_out, 0)
    r_io = lax.broadcasted_iota(jnp.int32, (n, n), 0)
    c_io = lax.broadcasted_iota(jnp.int32, (n, n), 1)
    place = ((0, 0), (1, 0), (1, HALF), (0, HALF))
    block = {(i, k): g_ref[place[i][0], :, place[i][1] + k * n:place[i][1] + (k + 1) * n]
             for k in range(count) for i in range(k, count)}
    low, xs = {}, []
    for k in range(count):
        v, u = eliminate(block[k, k], n, buf)
        factor[span(k), span(k)] = jnp.where(r_io >= c_io, u.T, 0.0)
        for i in range(k + 1, count):
            low[i, k] = full(block[i, k], v, NT)
            factor[span(i), span(k)] = low[i, k]
            factor[span(k), span(i)] = jnp.zeros((n, n), F32)
            if i == k + 1:
                block[i, i] = block[i, i] - full(low[i, k], low[i, k], NT)
        for i in range(k + 2, count):
            for j in range(k + 1, i + 1):
                block[i, j] = block[i, j] - full(low[i, k], low[j, k], NT)
        put(factor.at[span(k)], l_out.at[span(k)], 1 + k)
        acc = r_ref[span(k), :]
        for j in range(k):
            acc = acc - three(low[k, j], xs[j], NN)
        xs.append(three(v, acc, NN))
        dirs[span(k), :] = xs[k].astype(BF16)
        put(dirs.at[span(k)], d_out.at[span(k)], 1 + count + k)
    for copy in pending:
        copy.wait()


def shards(sides, basis_cols, snapshots):
    ny, nz, nx, points = sides
    own_points = basis_cols.shape[0] // nx
    modes = basis_cols.shape[1]
    snaps = snapshots.shape[0]
    n = max(ny, nz)
    dma = pltpu.SemaphoreType.DMA
    packed = (2, HALF // 2, HALF + snaps)

    def sum_buffers(rows, lanes):
        shapes = [(2, rows, lanes), (rows, lanes), (rows, lanes), (n, rows // n, lanes), (n, rows // n, lanes)]
        return [pltpu.VMEM(shape, F32) for shape in shapes]

    coefficients, gram, residual = pl.pallas_call(
        functools.partial(exchange, sides),
        out_shape=(
            jax.ShapeDtypeStruct((modes, snaps), F32),
            jax.ShapeDtypeStruct(packed, F32),
            jax.ShapeDtypeStruct((snaps, own_points), F32),
        ),
        in_specs=[pl.BlockSpec(memory_space=pltpu.HBM)] * 2,
        out_specs=(pl.BlockSpec(memory_space=pltpu.VMEM),) * 3,
        scratch_shapes=[
            pltpu.VMEM(basis_cols.shape, BF16),
            pltpu.VMEM(snapshots.shape, BF16),
            pltpu.VMEM((nx, own_points, modes), BF16),
            pltpu.VMEM((nx, snaps, modes), BF16),
            pltpu.VMEM((snaps, modes), F32),
            *sum_buffers(HALF, modes),
            *sum_buffers(*packed[1:]),
            pltpu.VMEM((nx, packed[1] // n, packed[2]), F32),
            pltpu.VMEM(packed, F32),
            dma((4,)),
            dma((len(SHARES), nx)), dma((len(SHARES), nx)),
            dma((2,)), dma((2,)),
            dma((2, n)), dma((2, n)),
            dma((2, n)), dma((2, n)),
            dma((2, nx)), dma((2, nx)),
            dma((2, n)), dma((2, n)),
            dma((2,)), dma((2,)),
            dma((n,)), dma((n,)),
            dma(()), dma(()),
        ],
        compiler_params=pltpu.CompilerParams(
            collective_id=0, has_side_effects=True, vmem_limit_bytes=52 << 20
        ),
        name="exchange",
    )(basis_cols, snapshots)
    block = 64
    coefficients, factor, directions = pl.pallas_call(
        functools.partial(factor_kernel, block),
        out_shape=(
            jax.ShapeDtypeStruct((modes, snaps), F32),
            jax.ShapeDtypeStruct((snaps, snaps), F32),
            jax.ShapeDtypeStruct((snaps, own_points), BF16),
        ),
        in_specs=[pl.BlockSpec(memory_space=pltpu.VMEM)] * 3,
        out_specs=(pl.BlockSpec(memory_space=pl.ANY),) * 3,
        scratch_shapes=[
            pltpu.VMEM((snaps, snaps), F32),
            pltpu.VMEM((snaps, own_points), BF16),
            pltpu.VMEM((2, 9, 8, 2 * block), F32),
            dma((1 + 2 * (snaps // block),)),
        ],
        compiler_params=pltpu.CompilerParams(vmem_limit_bytes=32 << 20),
        name="factor",
    )(gram, residual, coefficients)
    return (coefficients, factor, directions)


def solution(mesh):
    rows, cols = mesh.shape["rows"], mesh.shape["cols"]
    placed = (P("rows", "cols"), P(None, "rows"))

    def whole(basis_cols, snapshots):
        sides = (SIDE_Y, rows // (2 * SIDE_Y), cols, basis_cols.shape[0])
        return jax.shard_map(
            functools.partial(shards, sides),
            mesh=mesh,
            in_specs=placed,
            out_specs=(P("cols", None), P(), P(None, ("rows", "cols"))),
            check_vma=False,
        )(basis_cols, snapshots)

    return whole
```

```python
import functools
import math

import jax
import jax.numpy as jnp
from jax import lax
from jax.experimental import pallas as pl
from jax.experimental.pallas import tpu as pltpu
from jax.sharding import PartitionSpec as P

RANK = 1024
SIDE_Y = 8
MESH = pl.DeviceIdType.MESH
F32 = jnp.float32
BF16 = jnp.bfloat16
HALF = 128
SHARES = (8, 2, 4, 2)


def exchange(sides, b_hbm, s_hbm, coef_o, gram_o, res_o, bv, sv, bfull, qfull, cbuf, pbuf, psum,
             p_core, p_rs, p_ar, gbuf, gsum, g_core, g_rs, g_ar, x_in, gall, load_sem, bx_s, bx_r, core_s, core_r, rs_s, rs_r, ar_s, ar_r, x_s, x_r,
             ag_s, ag_r, out_s, out_r, cag_s, cag_r, cout_s, cout_r):
    ny, nz, nx, points = sides
    row, x = lax.axis_index("rows"), lax.axis_index("cols")
    z, y, c = row // (2 * ny), (row // 2) % ny, row % 2
    own_points = b_hbm.shape[0] // nx
    ring = ny
    rows = HALF // ring

    def device(z, y, c, x):
        return ((z * ny + y) * 2 + c, x)

    mate = device(z, y, 1 - c, x)
    far = sorted(range(1, ring), key=lambda k: -min(k, ring - k))
    one, two = jnp.where(c == 0, y, z), jnp.where(c == 0, z, y)
    one_peers = [lax.rem(one + k, ring) for k in far]
    two_peers = [lax.rem(two + k, ring) for k in far]
    x_peers = [lax.rem(x + k, nx) for k in sorted(range(1, nx), key=lambda k: -min(k, nx - k))]

    def along_one(t):
        return device(jnp.where(c == 0, z, t), jnp.where(c == 0, t, y), c, x)

    def along_two(t):
        return device(jnp.where(c == 0, t, z), jnp.where(c == 0, y, t), c, x)

    def along_x(t):
        return device(z, y, c, t)

    def remote(src, dst, send, recv, dev):
        return pltpu.make_async_remote_copy(
            src_ref=src, dst_ref=dst, send_sem=send, recv_sem=recv, device_id=dev, device_id_type=MESH
        )

    pending = []

    def send(*args):
        copy = remote(*args)
        copy.start()
        pending.append(copy)

    def arrived(ref, sem):
        remote(ref, ref, load_sem.at[3], sem, mate).wait_recv()

    load_b = pltpu.make_async_copy(b_hbm, bv, load_sem.at[0])
    load_s = pltpu.make_async_copy(s_hbm, sv, load_sem.at[1])
    load_b.start()
    load_s.start()

    barrier = pltpu.get_barrier_semaphore()
    peers = [mate] + [along_one(t) for t in one_peers] + [along_two(t) for t in two_peers]
    peers += [along_x(t) for t in x_peers]
    for peer in peers:
        pl.semaphore_signal(barrier, inc=1, device_id=peer, device_id_type=MESH)
    pl.semaphore_wait(barrier, len(peers))

    spans = [(sum(SHARES[:k]) * own_points // 16, SHARES[k] * own_points // 16) for k in range(len(SHARES))]

    def send_basis(k):
        start, size = spans[k]
        for t in x_peers:
            send(b_hbm.at[pl.ds(t * own_points + start, size)], bfull.at[x, pl.ds(start, size)], bx_s.at[k, t],
                 bx_r.at[k, x], along_x(t))

    send_basis(0)
    load_own = pltpu.make_async_copy(b_hbm.at[pl.ds(x * own_points, own_points)], bfull.at[x], load_sem.at[2])
    load_own.start()

    load_b.wait()
    load_s.wait()
    steps = 4
    depth = b_hbm.shape[0] // steps
    total = None
    for k in range(steps):
        piece = jnp.dot(sv[:, k * depth:(k + 1) * depth], bv[k * depth:(k + 1) * depth, :],
                        preferred_element_type=F32)
        total = piece if total is None else total + piece

    half = pl.ds(pl.multiple_of(c * HALF, HALF), HALF)
    other = pl.ds(pl.multiple_of((1 - c) * HALF, HALF), HALF)

    def half_chunk(t):
        return pl.ds(pl.multiple_of(c * HALF + t * rows, rows), rows)

    def row_sum(phase, own_sum, buf, core_in, rs_in, ar_in):
        send(buf.at[1 - c], core_in, core_s.at[phase], core_r.at[phase], mate)
        arrived(core_in, core_r.at[phase])
        own_sum[...] = buf[c] + core_in[...]
        size = own_sum.shape[0] // ring

        def piece(t):
            return pl.ds(pl.multiple_of(t * size, size), size)

        for t in one_peers:
            send(own_sum.at[piece(t)], rs_in.at[one], rs_s.at[phase, t], rs_r.at[phase, one], along_one(t))
        rs_in[one] = own_sum[piece(one), :]
        for t in one_peers:
            arrived(rs_in.at[t], rs_r.at[phase, t])
        got = rs_in[0]
        for i in range(1, ring):
            got = got + rs_in[i]
        ar_in[two] = got
        for t in two_peers:
            send(ar_in.at[two], ar_in.at[two], ar_s.at[phase, t], ar_r.at[phase, two], along_two(t))
        for t in two_peers:
            arrived(ar_in.at[t], ar_r.at[phase, t])
        got = ar_in[0]
        for i in range(1, ring):
            got = got + ar_in[i]
        return got

    pbuf[0], pbuf[1] = total[:HALF], total[HALF:]
    own = row_sum(0, psum, pbuf, p_core, p_rs, p_ar) * (math.sqrt(RANK) / points)
    mine = half_chunk(one)
    qfull[x, mine, :] = own.astype(BF16)
    for t in x_peers:
        send(qfull.at[x, mine], qfull.at[x, mine], x_s.at[0, t], x_r.at[0, x], along_x(t))
    send_basis(1)
    cbuf[mine, :] = own
    for t in x_peers:
        arrived(qfull.at[t, mine], x_r.at[0, t])
    for t in one_peers:
        send(qfull.at[:, mine], qfull.at[:, mine], ag_s.at[0, t], ag_r.at[0, one], along_one(t))
    for t in one_peers:
        send(cbuf.at[mine], cbuf.at[mine], cag_s.at[t], cag_r.at[one], along_one(t))
    send_basis(2)
    for t in one_peers:
        arrived(qfull.at[:, half_chunk(t)], ag_r.at[0, t])
    send(qfull.at[:, half], qfull.at[:, half], out_s.at[0], out_r.at[0], mate)
    send_basis(3)
    arrived(qfull.at[:, other], out_r.at[0])

    for t in one_peers:
        arrived(cbuf.at[half_chunk(t)], cag_r.at[t])
    send(cbuf.at[half], cbuf.at[half], cout_s, cout_r, mate)

    def sent():
        while pending:
            pending.pop().wait_send()

    load_own.wait()
    gram = None
    for k, (start, size) in enumerate(spans):
        recon = None
        for t in x_peers:
            arrived(bfull.at[t, pl.ds(start, size)], bx_r.at[k, t])
        for t in range(nx):
            piece = lax.dot_general(qfull[t], bfull[t, start:start + size, :], (((1,), (1,)), ((), ())),
                                    preferred_element_type=F32)
            recon = piece if recon is None else recon + piece
        snaps = sv[:, pl.ds(pl.multiple_of(x * own_points + start, math.gcd(start, size)), size)].astype(F32)
        residual = snaps - recon * (1.0 / math.sqrt(RANK))
        res_o[:, start:start + size] = residual
        piece = full(residual, residual, NT)
        gram = piece if gram is None else gram + piece
    gram = gram * (1.0 / points)
    q = HALF // 2
    for h, (top, low) in enumerate(((0, 3 * q), (q, HALF))):
        gbuf[h, :, :HALF] = gram[top:top + q, :HALF]
        gbuf[h, :, HALF:] = gram[low:low + q, :]
    got = row_sum(1, gsum, gbuf, g_core, g_rs, g_ar)
    x_in[x] = got
    for t in x_peers:
        send(x_in.at[x], x_in.at[x], x_s.at[1, t], x_r.at[1, x], along_x(t))
    arrived(cbuf.at[other], cout_r)
    coef_o[...] = cbuf[...].T
    sent()
    for t in x_peers:
        arrived(x_in.at[t], x_r.at[1, t])
    got = x_in[0]
    for i in range(1, nx):
        got = got + x_in[i]
    size = q // ring

    def gram_rows(t):
        return gall.at[c, pl.ds(pl.multiple_of(t * size, size), size)]

    gall[c, pl.ds(pl.multiple_of(one * size, size), size), :] = got
    for t in one_peers:
        send(gram_rows(one), gram_rows(one), ag_s.at[1, t], ag_r.at[1, one], along_one(t))
    for t in one_peers:
        arrived(gram_rows(t), ag_r.at[1, t])
    send(gall.at[c], gall.at[c], out_s.at[1], out_r.at[1], mate)
    gram_o[c] = gall[c]
    sent()
    arrived(gall.at[1 - c], out_r.at[1])
    gram_o[1 - c] = gall[1 - c]


def eliminate(a, n, buf):
    lanes = 2 * n
    count = n // 8
    r_io = lax.broadcasted_iota(jnp.int32, (8, n), 0)
    c_io = lax.broadcasted_iota(jnp.int32, (8, n), 1)
    sub = lax.broadcasted_iota(jnp.int32, (8, lanes), 0)
    tiles = [jnp.concatenate([jnp.where(c_io == r_io + 8 * t, 1.0, 0.0).astype(F32), a[8 * t:8 * t + 8]], axis=1)
             for t in range(count)]

    def spread(v):
        return jnp.broadcast_to(v, (8, lanes))

    for g in range(count):
        base, slot = n + 8 * g, g % 2
        cols = {t: [spread(tiles[t][:, base + k:base + k + 1]) for k in range(8)] for t in range(g, count)}
        for k in range(8):
            buf[slot, k] = cols[g][k]
        buf[slot, 8] = tiles[g]
        piv = [[spread(buf[slot, b, i:i + 1, :]) for b in range(i + 1)] for i in range(8)]
        rows = [spread(buf[slot, 8, k:k + 1, :]) for k in range(8)]
        for k in range(8):
            d = lax.rsqrt(piv[k][k])
            inv = pl.reciprocal(piv[k][k], approx=True)
            for i in range(k + 1, 8):
                for b in range(k + 1, i + 1):
                    piv[i][b] = piv[i][b] - (piv[i][k] * piv[b][k]) * inv
            low = {i: piv[i][k] * d for i in range(k + 1, 8)}
            rows[k] = rows[k] * d
            for i in range(k + 1, 8):
                rows[i] = rows[i] - low[i] * rows[k]
            for t in range(g + 1, count):
                cols[t][k] = cols[t][k] * d
                for i in range(k + 1, 8):
                    cols[t][i] = cols[t][i] - low[i] * cols[t][k]
                tiles[t] = tiles[t] - cols[t][k] * rows[k]
        new = rows[0]
        for k in range(1, 8):
            new = jnp.where(sub == k, rows[k], new)
        tiles[g] = new
    w = jnp.concatenate(tiles, axis=0)
    return w[:, :n], w[:, n:]


NN, NT = ((1,), (0,)), ((1,), (1,))


def split(v):
    high = v.astype(BF16)
    return high, (v - high.astype(F32)).astype(BF16)


def three(a, b, dims):
    (ah, al), (bh, bl) = split(a), split(b)

    def dot(p, q):
        return lax.dot_general(p, q, (dims, ((), ())), preferred_element_type=F32)

    return dot(ah, bh) + (dot(ah, bl) + dot(al, bh))


def full(a, b, dims):
    return lax.dot_general(a, b, (dims, ((), ())), precision=lax.Precision.HIGHEST, preferred_element_type=F32)


def factor_kernel(n, g_ref, r_ref, c_ref, c_out, l_out, d_out, factor, dirs, buf, sems):
    count = r_ref.shape[0] // n
    pending = []

    def put(src, dst, k):
        copy = pltpu.make_async_copy(src, dst, sems.at[k])
        copy.start()
        pending.append(copy)

    def span(k):
        return slice(k * n, (k + 1) * n)

    put(c_ref, c_out, 0)
    r_io = lax.broadcasted_iota(jnp.int32, (n, n), 0)
    c_io = lax.broadcasted_iota(jnp.int32, (n, n), 1)
    place = ((0, 0), (1, 0), (1, HALF), (0, HALF))
    block = {(i, k): g_ref[place[i][0], :, place[i][1] + k * n:place[i][1] + (k + 1) * n]
             for k in range(count) for i in range(k, count)}
    low, xs = {}, []
    for k in range(count):
        v, u = eliminate(block[k, k], n, buf)
        factor[span(k), span(k)] = jnp.where(r_io >= c_io, u.T, 0.0)
        for i in range(k + 1, count):
            low[i, k] = full(block[i, k], v, NT)
            factor[span(i), span(k)] = low[i, k]
            factor[span(k), span(i)] = jnp.zeros((n, n), F32)
            if i == k + 1:
                block[i, i] = block[i, i] - full(low[i, k], low[i, k], NT)
        for i in range(k + 2, count):
            for j in range(k + 1, i + 1):
                block[i, j] = block[i, j] - full(low[i, k], low[j, k], NT)
        put(factor.at[span(k)], l_out.at[span(k)], 1 + k)
        acc = r_ref[span(k), :]
        for j in range(k):
            acc = acc - three(low[k, j], xs[j], NN)
        xs.append(three(v, acc, NN))
        dirs[span(k), :] = xs[k].astype(BF16)
        put(dirs.at[span(k)], d_out.at[span(k)], 1 + count + k)
    for copy in pending:
        copy.wait()


def shards(sides, basis_cols, snapshots):
    ny, nz, nx, points = sides
    own_points = basis_cols.shape[0] // nx
    modes = basis_cols.shape[1]
    snaps = snapshots.shape[0]
    n = max(ny, nz)
    dma = pltpu.SemaphoreType.DMA
    packed = (2, HALF // 2, HALF + snaps)

    def sum_buffers(rows, lanes):
        shapes = [(2, rows, lanes), (rows, lanes), (rows, lanes), (n, rows // n, lanes), (n, rows // n, lanes)]
        return [pltpu.VMEM(shape, F32) for shape in shapes]

    coefficients, gram, residual = pl.pallas_call(
        functools.partial(exchange, sides),
        out_shape=(
            jax.ShapeDtypeStruct((modes, snaps), F32),
            jax.ShapeDtypeStruct(packed, F32),
            jax.ShapeDtypeStruct((snaps, own_points), F32),
        ),
        in_specs=[pl.BlockSpec(memory_space=pltpu.HBM)] * 2,
        out_specs=(pl.BlockSpec(memory_space=pltpu.VMEM),) * 3,
        scratch_shapes=[
            pltpu.VMEM(basis_cols.shape, BF16),
            pltpu.VMEM(snapshots.shape, BF16),
            pltpu.VMEM((nx, own_points, modes), BF16),
            pltpu.VMEM((nx, snaps, modes), BF16),
            pltpu.VMEM((snaps, modes), F32),
            *sum_buffers(HALF, modes),
            *sum_buffers(*packed[1:]),
            pltpu.VMEM((nx, packed[1] // n, packed[2]), F32),
            pltpu.VMEM(packed, F32),
            dma((4,)),
            dma((len(SHARES), nx)), dma((len(SHARES), nx)),
            dma((2,)), dma((2,)),
            dma((2, n)), dma((2, n)),
            dma((2, n)), dma((2, n)),
            dma((2, nx)), dma((2, nx)),
            dma((2, n)), dma((2, n)),
            dma((2,)), dma((2,)),
            dma((n,)), dma((n,)),
            dma(()), dma(()),
        ],
        compiler_params=pltpu.CompilerParams(
            collective_id=0, has_side_effects=True, vmem_limit_bytes=52 << 20
        ),
        name="exchange",
    )(basis_cols, snapshots)
    block = 64
    coefficients, factor, directions = pl.pallas_call(
        functools.partial(factor_kernel, block),
        out_shape=(
            jax.ShapeDtypeStruct((modes, snaps), F32),
            jax.ShapeDtypeStruct((snaps, snaps), F32),
            jax.ShapeDtypeStruct((snaps, own_points), BF16),
        ),
        in_specs=[pl.BlockSpec(memory_space=pltpu.VMEM)] * 3,
        out_specs=(pl.BlockSpec(memory_space=pl.ANY),) * 3,
        scratch_shapes=[
            pltpu.VMEM((snaps, snaps), F32),
            pltpu.VMEM((snaps, own_points), BF16),
            pltpu.VMEM((2, 9, 8, 2 * block), F32),
            dma((1 + 2 * (snaps // block),)),
        ],
        compiler_params=pltpu.CompilerParams(vmem_limit_bytes=32 << 20),
        name="factor",
    )(gram, residual, coefficients)
    return (coefficients, factor, directions)


def solution(mesh):
    rows, cols = mesh.shape["rows"], mesh.shape["cols"]
    placed = (P("rows", "cols"), P(None, "rows"))

    def whole(basis_cols, snapshots):
        sides = (SIDE_Y, rows // (2 * SIDE_Y), cols, basis_cols.shape[0])
        return jax.shard_map(
            functools.partial(shards, sides),
            mesh=mesh,
            in_specs=placed,
            out_specs=(P("cols", None), P(), P(None, ("rows", "cols"))),
            check_vma=False,
        )(basis_cols, snapshots)

    return whole
```
